32 devices in a mesh: section: 8 (over y, x, core), dp: 4 (over z).
Axes of the slice: x: 2, y: 2, z: 4, core: 2. Of those that a mesh axis runs over, the one named last changes fastest.
Arguments:
- tokens: bfloat16 [16, 32, 1024], P('dp'), may hold values from -6 to 6
- cotangent: bfloat16 [16, 32, 1024], P('dp'), may hold values from -6 to 6
- lengths: int32 [16, 4], P('dp'), may hold values from 1 to 16, 32 in all within a row
- mixer_gain: bfloat16 [16, 1024], P('section', 'dp'), may hold values from 0.5 to 1.5
- mixer_shift: bfloat16 [16, 1024], P('section', 'dp'), may hold values from -1.75 to 1.75
- input_weight: bfloat16 [16, 1024, 3072], P('section', 'dp'), may hold values from -0.1875 to 0.1875
- input_bias: bfloat16 [16, 3072], P('section', 'dp'), may hold values from -1.75 to 1.75
- short_kernel: bfloat16 [16, 3, 3072], P('section', None, 'dp'), may hold values from -3.5 to 3.5
- embed_weight: bfloat16 [16, 33, 64], P('section', None, 'dp'), may hold values from -1 to 1
- embed_bias: bfloat16 [16, 64], P('section', 'dp'), may hold values from -3.140625 to 3.140625
- filter_weight: bfloat16 [16, 64, 64], P('section', None, 'dp'), may hold values from -0.75 to 0.75
- filter_bias: bfloat16 [16, 64], P('section', 'dp'), may hold values from -3.140625 to 3.140625
- taps_weight: bfloat16 [16, 64, 1024], P('section', None, 'dp'), may hold values from -0.75 to 0.75
- skip_gain: bfloat16 [16, 1024], P('section', 'dp'), may hold values from -6 to 6
- output_weight: bfloat16 [16, 1024, 1024], P('section', 'dp'), may hold values from -0.09375 to 0.09375
- output_bias: bfloat16 [16, 1024], P('section', 'dp'), may hold values from -1.75 to 1.75
- feed_gain: bfloat16 [16, 1024], P('section', 'dp'), may hold values from 0.5 to 1.5
- feed_shift: bfloat16 [16, 1024], P('section', 'dp'), may hold values from -1.75 to 1.75
- up_weight: bfloat16 [16, 1024, 4096], P('section', 'dp'), may hold values from -0.1875 to 0.1875
- up_bias: bfloat16 [16, 4096], P('section', 'dp'), may hold values from -1.75 to 1.75
- down_weight: bfloat16 [16, 4096, 1024], P('section', 'dp'), may hold values from -0.09375 to 0.09375
- down_bias: bfloat16 [16, 1024], P('section', 'dp'), may hold values from -1.75 to 1.75
Outputs:
- section_out: float32 [8, 16, 32, 1024], P('section', 'dp')
- section_grad: float32 [8, 16, 32, 1024], P('section', 'dp')
- grad_mixer_gain: float32 [16, 1024], P('section', 'dp')
- grad_mixer_shift: float32 [16, 1024], P('section', 'dp')
- grad_input_weight: float32 [16, 1024, 3072], P('section', 'dp')
- grad_input_bias: float32 [16, 3072], P('section', 'dp')
- grad_short_kernel: float32 [16, 3, 3072], P('section', None, 'dp')
- grad_embed_weight: float32 [16, 33, 64], P('section', None, 'dp')
- grad_embed_bias: float32 [16, 64], P('section', 'dp')
- grad_filter_weight: float32 [16, 64, 64], P('section', None, 'dp')
- grad_filter_bias: float32 [16, 64], P('section', 'dp')
- grad_taps_weight: float32 [16, 64, 1024], P('section', None, 'dp')
- grad_skip_gain: float32 [16, 1024], P('section', 'dp')
- grad_output_weight: float32 [16, 1024, 1024], P('section', 'dp')
- grad_output_bias: float32 [16, 1024], P('section', 'dp')
- grad_feed_gain: float32 [16, 1024], P('section', 'dp')
- grad_feed_shift: float32 [16, 1024], P('section', 'dp')
- grad_up_weight: float32 [16, 1024, 4096], P('section', 'dp')
- grad_up_bias: float32 [16, 4096], P('section', 'dp')
- grad_down_weight: float32 [16, 4096, 1024], P('section', 'dp')
- grad_down_bias: float32 [16, 1024], P('section', 'dp')
The draws below stay inside these ranges and needn't reach their ends.
Inputs may be any that keep to these rules, and one draw needn't show every extreme that they name: Each row of lengths holds the lengths of 4 documents packed in order into one row of 32 tokens; they sum to 32, and some document in each row has 16 tokens.
All inputs are finite; a program needn't handle non-finite values.
Results may differ from the reference program's by a relative error of at most 0.033.
Values may be sent and summed in bfloat16 or wider, within the bound.
A program may use at most 256 MiB of HBM per device.

```python
import math
import jax
import jax.numpy as jnp
import numpy as np
from jax import lax

D = 1024
FF = 4096
FILT = 64
EMB = 33
NDOC = 4
MB_TOK = 32
ROWS = 16
LAYERS = 16
N_SECTION = 8


def block_scale(key, dims, shards, least, high):
    factor_of = 1.0
    for position, parts in shards:
        heights = jax.random.uniform(jax.random.fold_in(jax.random.fold_in(key, 6), position), (parts,), jnp.float32, least / len(shards), high / len(shards))
        factor_of = factor_of * jnp.repeat(jnp.exp(heights), dims[position] // parts).reshape((-1,) + (1,) * (len(dims) - 1 - position))
    return factor_of


def split_up(amount, total, limit, slope):
    weights = [(1 << 20) // math.isqrt(grade ** slope) + 1 for grade in range(2, amount + 1)]
    rest, given = total - limit - (amount - 1), [1] * (amount - 1)
    while rest > 0:
        free = [i for i in range(amount - 1) if given[i] < limit]
        pool, budget = sum([weights[i] for i in free]), rest
        for i in free:
            extra = min(limit - given[i], max(1, budget * weights[i] // pool), rest)
            given[i] = given[i] + extra
            rest = rest - extra
    return np.array([limit] + given)


def ragged(key, count, total, limit, lean):
    if count == 2:
        one = jax.random.randint(key, (), max(1, total - limit), min(limit, total - 1) + 1)
        return jnp.stack([one, total - one])
    sizes = jnp.asarray(split_up(count, total, limit, lean), jnp.int32)
    pairs = (count - 1) // 2
    giver, receiver = sizes[1:1 + 2 * pairs:2], sizes[2:2 + 2 * pairs:2]
    slack = jnp.minimum(giver - 1, limit - receiver)
    passed = jax.random.randint(jax.random.fold_in(key, 1), (pairs,), 0, 1 << 20) % (slack + 1)
    sizes = sizes.at[1:1 + 2 * pairs:2].set(giver - passed).at[2:2 + 2 * pairs:2].set(receiver + passed)
    return sizes[jax.random.permutation(jax.random.fold_in(key, 2), count)]


def normal_values(rng, shape, scale, bound, pieces=(), kind=jnp.bfloat16):
    values = jax.random.normal(rng, shape, jnp.float32) * scale
    if len(pieces) > 0:
        values = block_scale(rng, shape, pieces, -0.22, 0.18) * values
    return jnp.clip(values, min=-bound, max=bound).astype(kind)


def setup_inputs(seed: int = 0) -> dict:
    keys = jax.random.split(jax.random.key(seed), 23)
    tokens = normal_values(keys[0], (ROWS, MB_TOK, D), 1.0, 6.0, ((0, 4),))
    cotangent = normal_values(keys[1], (ROWS, MB_TOK, D), 1.0, 6.0, ((0, 4),))
    lengths = jax.vmap(lambda own: ragged(own, NDOC, MB_TOK, MB_TOK // 2, 2))(jax.random.split(keys[2], ROWS)).reshape((ROWS, NDOC)).astype(jnp.int32)
    mixer_gain = jnp.clip(1.0 + 0.1 * jax.random.normal(keys[3], (LAYERS, D), jnp.float32), 0.5, 1.5).astype(jnp.bfloat16)
    mixer_shift = normal_values(keys[4], (LAYERS, D), 0.3, 1.75, ((0, 8), (1, 4)))
    input_weight = normal_values(keys[5], (LAYERS, D, 3 * D), D ** -0.5, 0.1875, ((0, 8), (1, 4)))
    input_bias = normal_values(keys[6], (LAYERS, 3 * D), 0.3, 1.75, ((0, 8), (1, 4)))
    short_kernel = normal_values(keys[7], (LAYERS, 3, 3 * D), 3 ** -0.5, 3.5, ((0, 8), (2, 4)))
    embed_weight = normal_values(keys[8], (LAYERS, EMB, FILT), EMB ** -0.5, 1.0, ((0, 8), (2, 4)))
    embed_bias = jnp.clip(jax.random.uniform(keys[9], (LAYERS, FILT), jnp.float32, -3.140625, 3.140625), -3.140625, 3.140625).astype(jnp.bfloat16)
    filter_weight = normal_values(keys[10], (LAYERS, FILT, FILT), FILT ** -0.5, 0.75, ((0, 8), (2, 4)))
    filter_bias = jnp.clip(jax.random.uniform(keys[11], (LAYERS, FILT), jnp.float32, -3.140625, 3.140625), -3.140625, 3.140625).astype(jnp.bfloat16)
    taps_weight = normal_values(keys[12], (LAYERS, FILT, D), FILT ** -0.5, 0.75, ((0, 8), (2, 4)))
    skip_gain = normal_values(keys[13], (LAYERS, D), 1.0, 6.0, ((0, 8), (1, 4)))
    output_weight = normal_values(keys[14], (LAYERS, D, D), (4 * D) ** -0.5, 0.09375, ((0, 8), (1, 4)))
    output_bias = normal_values(keys[15], (LAYERS, D), 0.3, 1.75, ((0, 8), (1, 4)))
    feed_gain = jnp.clip(1.0 + 0.1 * jax.random.normal(keys[16], (LAYERS, D), jnp.float32), 0.5, 1.5).astype(jnp.bfloat16)
    feed_shift = normal_values(keys[17], (LAYERS, D), 0.3, 1.75, ((0, 8), (1, 4)))
    up_weight = normal_values(keys[18], (LAYERS, D, FF), D ** -0.5, 0.1875, ((0, 8), (1, 4)))
    up_bias = normal_values(keys[19], (LAYERS, FF), 0.3, 1.75, ((0, 8), (1, 4)))
    down_weight = normal_values(keys[20], (LAYERS, FF, D), FF ** -0.5, 0.09375, ((0, 8), (1, 4)))
    down_bias = normal_values(keys[21], (LAYERS, D), 0.3, 1.75, ((0, 8), (1, 4)))
    return {"tokens": tokens, "cotangent": cotangent, "lengths": lengths, "mixer_gain": mixer_gain, "mixer_shift": mixer_shift, "input_weight": input_weight, "input_bias": input_bias, "short_kernel": short_kernel, "embed_weight": embed_weight, "embed_bias": embed_bias, "filter_weight": filter_weight, "filter_bias": filter_bias, "taps_weight": taps_weight, "skip_gain": skip_gain, "output_weight": output_weight, "output_bias": output_bias, "feed_gain": feed_gain, "feed_shift": feed_shift, "up_weight": up_weight, "up_bias": up_bias, "down_weight": down_weight, "down_bias": down_bias}


@jax.custom_vjp
def low(v):
    return lax.optimization_barrier(v.astype(jnp.bfloat16)).astype(jnp.float32)

@jax.custom_vjp
def low_back(v):
    return v

def low_keep(v):
    return (low(v), None)

def low_pass(kept, grad):
    return (grad,)

def back_keep(v):
    return (v, None)

def back_low(kept, grad):
    return (low(grad),)
low.defvjp(low_keep, low_pass)
low_back.defvjp(back_keep, back_low)
EPSILON = 1e-05

def precise(left, right):
    return jnp.matmul(left, right, precision=lax.Precision.HIGHEST)

def layer_norm(value, gain, shift):
    centre = lax.optimization_barrier(jnp.mean(value, axis=-1, keepdims=True))
    centred = value - centre
    spread = lax.optimization_barrier(jnp.mean(centred * centred, axis=-1, keepdims=True))
    return centred * lax.rsqrt(spread + EPSILON) * gain + shift

def positions(length, width):
    steps = jnp.arange(length, dtype=jnp.float32)
    bands = jnp.arange(1, 17, dtype=jnp.float32)
    angles = 2.0 * jnp.pi * steps[:, None] * bands[None, :] / length
    table = jnp.concatenate([(steps / length)[:, None], jnp.cos(angles), jnp.sin(angles)], axis=1)
    rates = jnp.exp(jnp.linspace(math.log(0.3), math.log(30.0), width)).astype(jnp.float32)
    decay = jnp.exp(-(steps / length)[:, None] * rates[None, :])
    return (table, decay)

def filter_taps(embed_weight, embed_bias, filter_weight, filter_bias, taps_weight, length):
    table, decay = positions(length, taps_weight.shape[-1])
    first = jnp.sin(precise(table, embed_weight) + embed_bias)
    second = jnp.sin(precise(first, filter_weight) + filter_bias)
    return precise(second, taps_weight) * decay

def segment_ids(lengths, length):
    ends = jnp.cumsum(lengths, axis=-1).astype(jnp.int32)
    steps = jnp.arange(length, dtype=jnp.int32)
    return lax.optimization_barrier(jnp.sum((steps[..., :, None] >= ends[..., None, :]).astype(jnp.int32), axis=-1)).astype(jnp.int32)

def shift_rows(value, offset):
    length = value.shape[-2]
    padded = jnp.concatenate([jnp.zeros_like(value), value], axis=-2)
    return lax.dynamic_slice_in_dim(padded, length - offset, length, axis=-2)

def shift_ids(segments, offset):
    length = segments.shape[-1]
    padded = jnp.concatenate([jnp.full_like(segments, -1), segments], axis=-1)
    return lax.dynamic_slice_in_dim(padded, length - offset, length, axis=-1)

def mixer(project, short_kernel, taps, skip_gain, segments):
    length = project.shape[-2]
    convolved = short_kernel[0] * project
    for offset in (1, 2):
        same_doc = (segments == shift_ids(segments, offset))[..., None]
        convolved = convolved + short_kernel[offset] * jnp.where(same_doc, shift_rows(project, offset), 0.0)
    width = project.shape[-1] // 3
    gate_out = convolved[..., :width]
    gate_in = convolved[..., width:2 * width]
    values = convolved[..., 2 * width:]
    mixed = values * gate_in

    def lag_step(total, pair):
        offset, tap_row = pair
        same_doc = (segments == shift_ids(segments, offset))[..., None]
        return (total + tap_row * jnp.where(same_doc, shift_rows(mixed, offset), 0.0), None)
    longconv, _ = lax.scan(jax.checkpoint(lag_step), skip_gain * mixed, (jnp.arange(length, dtype=jnp.int32), taps))
    return longconv * gate_out

def layer(stream, weights, taps, segments):
    mixer_gain, mixer_shift, input_weight, input_bias, short_kernel, skip_gain, output_weight, output_bias, feed_gain, feed_shift, up_weight, up_bias, down_weight, down_bias = weights
    normed = low(layer_norm(stream, mixer_gain, mixer_shift))
    project = low_back(precise(normed, input_weight)) + input_bias
    gated = low(mixer(project, short_kernel, taps, skip_gain, segments))
    middle = stream + low_back(precise(gated, output_weight)) + output_bias
    second = low(layer_norm(middle, feed_gain, feed_shift))
    before = low_back(precise(second, up_weight)) + up_bias
    activated = low(jax.nn.gelu(before, approximate=False))
    return middle + low_back(precise(activated, down_weight)) + down_bias

def reference(tokens, cotangent, lengths, mixer_gain, mixer_shift, input_weight, input_bias, short_kernel, embed_weight, embed_bias, filter_weight, filter_bias, taps_weight, skip_gain, output_weight, output_bias, feed_gain, feed_shift, up_weight, up_bias, down_weight, down_bias):
    segments = segment_ids(lengths, MB_TOK)
    weights = tuple((piece.astype(jnp.float32) for piece in (mixer_gain, mixer_shift, input_weight, input_bias, short_kernel, embed_weight, embed_bias, filter_weight, filter_bias, taps_weight, skip_gain, output_weight, output_bias, feed_gain, feed_shift, up_weight, up_bias, down_weight, down_bias)))
    start = tokens.astype(jnp.float32)
    probes = jnp.zeros((N_SECTION,) + tokens.shape, jnp.float32)

    def forward(start, probes, weights):
        stream = start
        results = []
        for section_index in range(N_SECTION):
            stream = stream + probes[section_index]
            for inner in range(2):
                index = 2 * section_index + inner
                take = tuple((piece[index] for piece in weights))
                taps = filter_taps(take[5], take[6], take[7], take[8], take[9], MB_TOK)
                layer_weights = (take[0], take[1], take[2], take[3], take[4], take[10], take[11], take[12], take[13], take[14], take[15], take[16], take[17], take[18])
                stream = jax.checkpoint(layer)(stream, layer_weights, taps, segments)
            results.append(stream)
        return (stream, jnp.stack(results))
    final, vjp_function, hidden = jax.vjp(forward, start, probes, weights, has_aux=True)
    grad_start, grad_probes, grad_weights = vjp_function(cotangent.astype(jnp.float32))
    return (hidden, grad_probes) + tuple(grad_weights)
```

```python
import functools
import math

import jax
import jax.numpy as jnp
import numpy as np
from jax import lax
from jax.experimental import pallas as pl
from jax.experimental.pallas import tpu as pltpu
from jax.sharding import PartitionSpec as P

EPSILON = 1e-05
MESH = pl.DeviceIdType.MESH
F32 = jnp.float32
BF16 = jnp.bfloat16
PLANES = 4
SMALL = 32
HIGH = lax.Precision.HIGHEST
HOPS = 4


def div(a, b):
    return lax.div(a, jnp.int32(b))


def rem(a, b):
    return lax.rem(a, jnp.int32(b))


def bits(count):
    return max(0, (count - 1).bit_length())


def gray(p, count):
    if count & (count - 1):
        return p
    return sum(
        (2**b * rem(rem(div(p, 2**b), 2) + rem(div(p, 2 ** (b + 1)), 2), 2) for b in range(bits(count))),
        jnp.int32(0),
    )


def ungray(c, count):
    if count & (count - 1):
        return c
    total = jnp.int32(0)
    for b in range(bits(count)):
        upper = sum((rem(div(c, 2**q), 2) for q in range(b, bits(count))), jnp.int32(0))
        total = total + 2**b * rem(upper, 2)
    return total


def snake(p, group, count):
    back = rem(group, 2)
    return p + back * (count - 1 - 2 * p)


def column_of(layer, columns):
    group = div(layer, columns)
    return gray(snake(rem(layer, columns), group, columns), columns)


def plane_of(layer, columns):
    return rem(div(layer, columns) + 1, PLANES)


def layer_of(column, plane, columns):
    group = rem(plane + PLANES - 1, PLANES)
    return group * columns + snake(ungray(column, columns), group, columns)


def fold(value):
    total = value[0:8]
    for step in range(8, value.shape[0], 8):
        total = total + value[step : step + 8]
    return total


def norm_parts(value):
    centred = value - jnp.mean(value, axis=-1, keepdims=True)
    rate = lax.rsqrt(jnp.mean(centred * centred, axis=-1, keepdims=True) + EPSILON)
    return centred * rate, rate


def norm_back(grad, gain, unit, rate):
    inner = grad * gain
    first = jnp.mean(inner, axis=-1, keepdims=True)
    second = jnp.mean(inner * unit, axis=-1, keepdims=True)
    return rate * (inner - first - unit * second)


def dot_right(left, right):
    return lax.dot_general(left, right, (((1,), (1,)), ((), ())), preferred_element_type=F32)


def dot_tokens(left, right, precision=None):
    return lax.dot_general(
        left, right, (((0,), (0,)), ((), ())), precision=precision, preferred_element_type=F32
    )


def kernel(
    size,
    tokens,
    cotangent,
    in_w,
    out_w,
    up_w,
    down_w,
    lengths,
    vectors,
    input_bias,
    short_kernel,
    up_bias,
    taps_weight,
    embed_weight,
    embed_bias,
    filter_weight,
    filter_bias,
    decay,
    table,
    g_in_w,
    g_out_w,
    g_up_w,
    g_down_w,
    g_small,
    g_filt,
    r_out,
    r_grad,
    rel,
    rel_down,
    back,
    back_down,
    w,
    sm,
    ft,
    own_sm,
    own_ft,
    own_mask,
    square,
    v1,
    bi,
    ks,
    bu,
    tw,
    taps,
    fstate,
    bm,
    s_in,
    g_arr,
    s_out,
    g_out,
    xn,
    xg,
    x2,
    xa,
    proj,
    conv,
    lcs,
    gpr,
    mid,
    dp,
    dg,
    dh,
    pxn,
    pxg,
    px2,
    pxa,
    pdp,
    pdg,
    pdh,
    pdm,
    a1,
    abi,
    aks,
    abu,
    atp,
    sgrad,
    fgrad,
    ws,
    rr,
    ls,
    wr,
    fs,
    fr,
    ps,
    pr,
    ms,
    mr,
    ts,
    cs,
    hfs,
    hfr,
    hbs,
    hbr,
    sos,
    sor,
    sgs,
    sgr,
    xs,
    xr,
    ds,
    dr,
    gs,
    gr,
    br,
    bs,
    vs,
    vr,
    lag_sem,
):
    S, n, R, D, FF, m, MT, lags, units, length = size
    C = S // 2
    dn, fn, un = D // n, FF // n, units // n
    h, fh = dn // 2, fn // 2
    wide = FF // D
    blocks = 4 + wide
    pieces = blocks + 1
    layers = PLANES * C
    s, z = lax.axis_index("section"), lax.axis_index("dp")
    k, c = rem(s, 2), div(s, 2)
    rho, plane = div(z, PLANES), rem(z, PLANES)
    other = s + 1 - 2 * k
    layer = layer_of(c, plane, C)
    own_s, own_e = div(layer, 2), rem(layer, 2)
    first, last = layer == 0, layer == layers - 1

    def chip_of(stage):
        return 2 * column_of(stage, C) + k, PLANES * rho + plane_of(stage, C)

    next_s, next_z = chip_of(jnp.minimum(layer + 1, layers - 1))
    prev_s, prev_z = chip_of(jnp.maximum(layer - 1, 0))

    def remote(src, dst, send, recv, to_s, to_z):
        return pltpu.make_async_remote_copy(
            src_ref=src,
            dst_ref=dst,
            send_sem=send,
            recv_sem=recv,
            device_id=(to_s, to_z),
            device_id_type=MESH,
        )

    def start(src, dst, send, recv, to_s, to_z, when=True):
        here = jnp.logical_and(to_s == s, to_z == z)

        @pl.when(jnp.logical_and(when, here))
        def _():
            pltpu.make_async_copy(src, dst, recv).start()

        @pl.when(jnp.logical_and(when, jnp.logical_not(here)))
        def _():
            remote(src, dst, send, recv, to_s, to_z).start()

    def sent(src, dst, send, recv, to_s, to_z, when=True):
        here = jnp.logical_and(to_s == s, to_z == z)

        @pl.when(jnp.logical_and(when, jnp.logical_not(here)))
        def _():
            remote(src, dst, send, recv, to_s, to_z).wait_send()

    def arrived(dst, recv):
        remote(dst, dst, recv, recv, other, z).wait_recv()

    def rows(index, count):
        return pl.ds(pl.multiple_of(index * count, count), count)

    barrier = pltpu.get_barrier_semaphore()

    @pl.loop(0, S)
    def _(a):
        @pl.loop(0, n)
        def _(b):
            @pl.when(jnp.logical_or(a != s, b != z))
            def _():
                pl.semaphore_signal(barrier, inc=1, device_id=(a, b), device_id_type=MESH)

    pl.semaphore_wait(barrier, S * n - 1)

    def relay_at(group, pos):
        return rel.at[group, pos] if pos < blocks else rel_down.at[group]

    def held_at(pos, q, core):
        if pos < blocks:
            return w.at[pos, rows(2 * q + core, h)]
        begin = q * fn + core * fh
        return w.at[blocks + div(begin, D), pl.ds(pl.multiple_of(rem(begin, D), fh), fh)]

    def source_at(e, core, pos):
        strip = pl.ds(core * h, h)
        if pos < 3:
            return in_w.at[e, strip, pl.ds(pos * D, D)]
        if pos == 3:
            return out_w.at[e, strip]
        if pos < blocks:
            return up_w.at[e, strip, pl.ds((pos - 4) * D, D)]
        return down_w.at[e, pl.ds(core * fh, fh)]

    def column_copies():
        for pos in range(pieces):
            for e in range(2):
                lay = 2 * s + e
                to_c, group = column_of(lay, C), div(lay, C)
                for core in range(2):
                    yield (
                        source_at(e, core, pos),
                        relay_at(group, pos),
                        ws.at[e, core, pos],
                        rr.at[group, pos],
                        2 * to_c + core,
                        z,
                    )

    def plane_copies(group, pos):
        to_p = (group + 1) % PLANES
        for copy in range(R):
            yield (
                relay_at(group, pos),
                held_at(pos, z, k),
                ls.at[group, copy, pos],
                wr.at[pos, z],
                s,
                PLANES * copy + to_p,
            )

    def pass_on(group, pos):
        arrived(relay_at(group, pos), rr.at[group, pos])
        for copy in plane_copies(group, pos):
            start(*copy)

    first_s, first_z = chip_of(jnp.int32(0))
    last_s, last_z = chip_of(jnp.int32(layers - 1))
    HW = D // HOPS

    def token_copies():
        at = rows(plane, MT)
        for part in range(HOPS):
            col = pl.ds(part * HW, HW)
            yield (
                tokens.at[rows(k, MT), col],
                s_in.at[at, col],
                ts.at[part],
                hfr.at[plane, part],
                first_s,
                first_z,
                s == first_s,
            )
        yield (
            cotangent.at[rows(k, MT)],
            g_arr.at[at],
            cs.at[0],
            hbr.at[plane],
            last_s,
            last_z,
            s == last_s,
        )

    def small_copies():
        for q in range(PLANES):
            yield (own_mask, bm.at[rows(plane, MT)], ms.at[q], mr.at[plane], s, PLANES * rho + q, True)
        for e in range(2):
            lay = 2 * s + e
            to_c, to_p = column_of(lay, C), plane_of(lay, C)
            for copy in range(R):
                to_z = PLANES * copy + to_p
                for core in range(2):
                    to = 2 * to_c + core
                    yield (own_sm.at[e], sm.at[z], ps.at[0, e, copy, core], pr.at[0, z], to, to_z)
                    yield (
                        own_ft.at[e],
                        ft.at[rows(z, un)],
                        ps.at[1, e, copy, core],
                        pr.at[1, z],
                        to,
                        to_z,
                    )

    for copy in token_copies():
        start(*copy)
    for copy in column_copies():
        start(*copy)

    step = lax.broadcasted_iota(jnp.int32, (length, 128), 0)
    for r in range(MT // length):
        begins = step == 0
        begin = jnp.int32(0)
        for doc in range(lengths.shape[1]):
            begin = begin + lengths[k * (MT // length) + r, doc]
            begins = jnp.logical_or(begins, step == begin)
        own_mask[r * length : (r + 1) * length, :] = jnp.where(begins, 0.0, 1.0)

    own_sm[...] = jnp.zeros_like(own_sm)
    for index in range(7):
        own_sm[:, index, :] = vectors[index, :, :].astype(F32)
    wide_bias, wide_up = input_bias[...].astype(F32), up_bias[...].astype(F32)
    for r in range(3):
        own_sm[:, 7 + r, :] = wide_bias[:, r * dn : (r + 1) * dn]
        for e in range(2):
            three = short_kernel[e].astype(F32)
            for tap in range(3):
                own_sm[e, 10 + 3 * tap + r, :] = three[tap, r * dn : (r + 1) * dn]
    for r in range(wide):
        own_sm[:, 19 + r, :] = wide_up[:, r * dn : (r + 1) * dn]
    own_sm[:, SMALL:, :] = taps_weight[...].astype(F32)
    for net, (weight, bias) in enumerate(((embed_weight, embed_bias), (filter_weight, filter_bias))):
        depth = weight.shape[1]
        for e in range(2):
            square[...] = jnp.zeros_like(square)
            square[0:depth, 0:un] = weight[e].astype(F32)
            square[depth : depth + 1, 0:un] = bias[e : e + 1, :].astype(F32)
            own_ft[e, :, net * 128 : (net + 1) * 128] = square[...].T[0:un, :]
    for copy in small_copies():
        start(*copy)

    ft[pl.ds(units, units), :] = jnp.zeros((units, 256), F32)
    a1[...] = jnp.zeros_like(a1)
    abi[...] = jnp.zeros_like(abi)
    aks[...] = jnp.zeros_like(aks)
    abu[...] = jnp.zeros_like(abu)
    atp[...] = jnp.zeros_like(atp)
    sgrad[...] = jnp.zeros_like(sgrad)

    for pos in range(pieces):
        for group in (0, 1):
            pass_on(group, pos)
        for near, group in ((1, 3), (2, 2)):

            @pl.when(plane == near)
            def _():
                pass_on(group, pos)

    defers = layer == C - 1

    def pass_rest():
        for pos in range(pieces):
            for near, group in ((1, 3), (2, 2)):

                @pl.when(plane != near)
                def _():
                    pass_on(group, pos)

    @pl.when(jnp.logical_not(defers))
    def _():
        pass_rest()

    @pl.loop(0, n)
    def _(q):
        arrived(sm.at[q], pr.at[0, q])
        arrived(ft.at[rows(q, un)], pr.at[1, q])

    for q in range(n):
        block = sm[q, 0:SMALL, :]
        v1[:, q * dn : (q + 1) * dn] = block[0:8]
        for r in range(3):
            at = slice((3 * q + r) * dn, (3 * q + r + 1) * dn)
            bi[0:1, at] = block[7 + r : 8 + r]
            for tap in range(3):
                ks[tap : tap + 1, at] = block[10 + 3 * tap + r : 11 + 3 * tap + r]
        for r in range(wide):
            at = slice((wide * q + r) * dn, (wide * q + r + 1) * dn)
            bu[0:1, at] = block[19 + r : 20 + r]
        tw[:, q * dn : (q + 1) * dn] = sm[q, SMALL : SMALL + units, :]

    lane = lax.broadcasted_iota(jnp.int32, (lags, 2 * units), 1)
    embed, deep = ft[:, 0:128], ft[:, 128:256]
    pre1 = lax.dot_general(
        table[...], embed, (((1,), (1,)), ((), ())), precision=HIGH, preferred_element_type=F32
    )
    one = jnp.where(lane == units, 1.0, jnp.sin(pre1))
    pre2 = lax.dot_general(
        one, deep, (((1,), (1,)), ((), ())), precision=HIGH, preferred_element_type=F32
    )
    two = jnp.sin(pre2)
    fstate[0] = one
    fstate[1] = jnp.cos(pre1)
    fstate[2] = two
    fstate[3] = jnp.cos(pre2)
    taps[...] = (
        jnp.dot(two[:, 0:units], tw[...], precision=HIGH, preferred_element_type=F32) * decay[...]
    )

    @pl.loop(0, PLANES)
    def _(q):
        arrived(bm.at[rows(q, MT)], mr.at[q])

    def share_copy(pos, q):
        at = held_at(pos, q, k)
        return remote(at, at, fs.at[pos, q], fr.at[pos, q], other, z)

    @pl.loop(0, n)
    def _(q):
        for pos in range(pieces):
            arrived(held_at(pos, q, k), wr.at[pos, q])
            share_copy(pos, q).start()

    @pl.loop(0, n)
    def _(q):
        for pos in range(pieces):
            share_copy(pos, q).wait()

    CB = 256
    UB = 512
    per = D // UB

    def spread(block, width):
        return jnp.concatenate([block] * (width // 128), axis=1)

    def hop_forward(b, part):
        at, col = rows(b, MT), pl.ds(part * HW, HW)
        return remote(
            s_out.at[at, col], s_in.at[at, col], hfs.at[b, part], hfr.at[b, part], next_s, next_z
        )

    def give_out(b):
        return (
            s_out.at[rows(b, MT)],
            r_out.at[rows(k, MT)],
            sos.at[b],
            sor.at[k],
            own_s,
            PLANES * rho + b,
            own_e == 1,
        )

    def give_grad(b):
        return (
            g_out.at[rows(b, MT)],
            r_grad.at[rows(k, MT)],
            sgs.at[b],
            sgr.at[k],
            own_s,
            PLANES * rho + b,
            own_e == 0,
        )

    halves = ((xn, pxn, D // 2), (xg, pxg, D // 2), (x2, px2, D // 2), (xa, pxa, FF // 2))

    def swap_left(b, pos):
        src, dst, width = halves[pos]
        at = rows(b, MT)
        return remote(
            src.at[at, rows(1 - k, width)], dst.at[at], xs.at[pos, b], xr.at[pos, b], other, z
        )

    fulls = ((dp, pdp), (dg, pdg), (dh, pdh), (g_arr, pdm))

    def swap_right(b, pos):
        src, dst = fulls[pos]
        at = rows(b, MT)
        return remote(src.at[at], dst.at[at], ds.at[pos, b], dr.at[pos, b], other, z)

    @pl.when(jnp.logical_and(first, k == 0))
    def _():
        pl.semaphore_signal(lag_sem, inc=1, device_id=(other, z), device_id_type=MESH)

    @pl.when(jnp.logical_and(first, k == 1))
    def _():
        pl.semaphore_wait(lag_sem, 1)

    @pl.loop(0, m)
    def _(b):
        at = rows(b, MT)
        for part in range(HOPS):
            arrived(s_in.at[at, pl.ds(part * HW, HW)], hfr.at[b, part])
        stream = s_in[at, :].astype(F32)
        unit, _ = norm_parts(stream)
        normed = (unit * v1[0:1, :] + v1[1:2, :]).astype(BF16)
        xn[at, :] = normed
        bb = spread(bm[at, :], CB)
        for cb in range(D // CB):
            col = slice(cb * CB, (cb + 1) * CB)
            parts = []
            for group in range(3):
                wcol = slice(group * D + cb * CB, group * D + (cb + 1) * CB)
                p = jnp.dot(normed, w[group, :, col], preferred_element_type=F32) + bi[0:1, wcol]
                y1 = bb * pltpu.roll(p, 1, 0)
                y2 = bb * pltpu.roll(y1, 1, 0)
                out = ks[0:1, wcol] * p + ks[1:2, wcol] * y1 + ks[2:3, wcol] * y2
                proj[at, wcol] = p
                conv[at, wcol] = out
                parts.append(out)
            mixed = parts[2] * parts[1]
            total = (v1[2:3, col] + taps[0:1, col]) * mixed
            moved = mixed
            for lag in range(1, lags):
                moved = bb * pltpu.roll(moved, 1, 0)
                total = total + taps[lag : lag + 1, col] * moved
            lcs[at, col] = total
            xg[at, col] = (total * parts[0]).astype(BF16)
        gated = xg[at, :]
        for cb in range(D // CB):
            col = slice(cb * CB, (cb + 1) * CB)
            mid[at, col] = (
                s_in[at, col].astype(F32)
                + jnp.dot(gated, w[3, :, col], preferred_element_type=F32)
                + v1[3:4, col]
            )
        unit, _ = norm_parts(mid[at, :])
        second = (unit * v1[4:5, :] + v1[5:6, :]).astype(BF16)
        x2[at, :] = second
        for ub in range(FF // UB):
            col = slice(ub * UB, (ub + 1) * UB)
            wcol = slice((ub % per) * UB, (ub % per + 1) * UB)
            before = (
                jnp.dot(second, w[4 + ub // per, :, wcol], preferred_element_type=F32) + bu[0:1, col]
            )
            phi = 0.5 + 0.5 * lax.erf(before * (1.0 / math.sqrt(2.0)))
            dens = jnp.exp(-0.5 * before * before) * (1.0 / math.sqrt(2.0 * math.pi))
            gpr[at, col] = phi + before * dens
            xa[at, col] = (before * phi).astype(BF16)
        for part in range(HOPS):
            col = slice(part * HW, (part + 1) * HW)
            total = mid[at, col] + v1[6:7, col]
            for q in range(wide):
                total = total + jnp.dot(
                    xa[at, q * D : (q + 1) * D], w[blocks + q, :, col], preferred_element_type=F32
                )
            s_out[at, col] = total.astype(BF16)

            @pl.when(jnp.logical_not(last))
            def _():
                hop_forward(b, part).start()

        start(*give_out(b))
        for pos in range(4):
            swap_left(b, pos).start()

    @pl.when(defers)
    def _():
        pass_rest()

    TB = 256

    @pl.loop(0, blocks + wide)
    def _(b):
        for top in range(D // TB):
            up = slice(top * TB, (top + 1) * TB)
            w[b, up, up] = w[b, up, up].T
            for low in range(top + 1, D // TB):
                down = slice(low * TB, (low + 1) * TB)
                one, two = w[b, up, down], w[b, down, up]
                w[b, up, down] = two.T
                w[b, down, up] = one.T

    def hop_back(b):
        at = rows(b, MT)
        return remote(g_out.at[at], g_arr.at[at], hbs.at[b], hbr.at[b], prev_s, prev_z)

    @pl.when(jnp.logical_and(last, k == 0))
    def _():
        pl.semaphore_signal(lag_sem, inc=1, device_id=(other, z), device_id_type=MESH)

    @pl.when(jnp.logical_and(last, k == 1))
    def _():
        pl.semaphore_wait(lag_sem, 1)

    @pl.loop(0, m)
    def _(b):
        at = rows(b, MT)
        arrived(g_arr.at[at], hbr.at[b])
        swap_right(b, 3).start()
        low = g_arr[at, :]
        grad = low.astype(F32)
        a1[6] += fold(grad)
        for ub in range(FF // UB):
            col = slice(ub * UB, (ub + 1) * UB)
            wcol = slice((ub % per) * UB, (ub % per + 1) * UB)
            inner = (
                jnp.dot(low, w[blocks + ub // per, :, wcol], preferred_element_type=F32)
                * gpr[at, col]
            )
            abu[:, col] += fold(inner)
            dh[at, col] = inner.astype(BF16)
        swap_right(b, 2).start()

        def times(left, begin, count):
            parts = []
            for cb in range(D // CB):
                col = slice(cb * CB, (cb + 1) * CB)
                parts.append(
                    sum(
                        jnp.dot(
                            left[at, q * D : (q + 1) * D],
                            w[begin + q, :, col],
                            preferred_element_type=F32,
                        )
                        for q in range(count)
                    )
                )
            return jnp.concatenate(parts, axis=1)

        grad2 = times(dh, 4, wide)
        unit, rate = norm_parts(mid[at, :])
        a1[4] += fold(grad2 * unit)
        a1[5] += fold(grad2)
        middle = grad + norm_back(grad2, v1[4:5, :], unit, rate)
        a1[3] += fold(middle)
        mid[at, :] = middle
        low = middle.astype(BF16)
        dg[at, :] = low
        swap_right(b, 1).start()
        bb = bm[at, :]
        bb = spread(pltpu.roll(bb, MT - 1, 0), CB)
        for cb in range(D // CB):
            col = slice(cb * CB, (cb + 1) * CB)
            gg = jnp.dot(low, w[3, :, col], preferred_element_type=F32)
            cols = [slice(g * D + cb * CB, g * D + (cb + 1) * CB) for g in range(3)]
            c_out, c_in, c_val = (conv[at, item] for item in cols)
            d_out = gg * lcs[at, col]
            moved = gg * c_out
            mixed = c_in * c_val
            direct = fold(moved * mixed)
            a1[2, :, col] += direct
            atp[0, :, col] += direct
            total = (v1[2:3, col] + taps[0:1, col]) * moved
            for lag in range(1, lags):
                moved = bb * pltpu.roll(moved, MT - 1, 0)
                total = total + taps[lag : lag + 1, col] * moved
                atp[lag, :, col] += fold(moved * mixed)
            for item, piece in zip(cols, (d_out, total * c_val, total * c_in)):
                z1 = bb * pltpu.roll(piece, MT - 1, 0)
                z2 = bb * pltpu.roll(z1, MT - 1, 0)
                p = proj[at, item]
                whole = ks[0:1, item] * piece + ks[1:2, item] * z1 + ks[2:3, item] * z2
                aks[0, :, item] += fold(p * piece)
                aks[1, :, item] += fold(p * z1)
                aks[2, :, item] += fold(p * z2)
                abi[:, item] += fold(whole)
                dp[at, item] = whole.astype(BF16)
        swap_right(b, 0).start()
        grad1 = times(dp, 0, 3)
        unit, rate = norm_parts(s_in[at, :].astype(F32))
        a1[0] += fold(grad1 * unit)
        a1[1] += fold(grad1)
        g_out[at, :] = (mid[at, :] + norm_back(grad1, v1[0:1, :], unit, rate)).astype(BF16)

        @pl.when(jnp.logical_not(first))
        def _():
            hop_back(b).start()

        start(*give_grad(b))

    @pl.loop(0, m)
    def _(b):
        for pos in range(4):
            swap_left(b, pos).wait()
            swap_right(b, pos).wait()

    def made_at(pos, q):
        if pos < blocks:
            return pos, q * dn
        return blocks + div(q * fn, D), rem(q * fn, D)

    def home_at(e, copy, pos):
        if pos < 3:
            return g_in_w.at[e, copy, :, pl.ds(pos * D, D)]
        if pos == 3:
            return g_out_w.at[e, copy]
        if pos < blocks:
            return g_up_w.at[e, copy, :, pl.ds((pos - 4) * D, D)]
        return g_down_w.at[e, copy]

    def back_at(group, copy, pos):
        return back.at[group, copy, pos] if pos < blocks else back_down.at[group, copy]

    own_group = div(layer, C)
    relayed = own_group >= 2

    def made(pos, half):
        q = k * (n // 2) + half
        block, begin = made_at(pos, q)
        share = dn if pos < blocks else fn
        return q, w.at[block, pl.ds(pl.multiple_of(begin, share), share)]

    def relay_copy(pos, half):
        q, src = made(pos, half)
        to = jnp.maximum(own_group - 2, 0)
        return (
            src,
            back_at(to, rho, pos),
            gs.at[pos, half],
            br.at[to, rho, pos],
            2 * c + rem(own_s, 2),
            q,
            relayed,
        )

    def direct_copy(pos, half):
        q, src = made(pos, half)
        return (
            src,
            home_at(own_e, rho, pos),
            gs.at[pos, half],
            gr.at[pos, own_e, rho],
            own_s,
            q,
            jnp.logical_not(relayed),
        )

    def home_copy(group, copy, pos):
        lay = layer_of(c, jnp.int32((group + 3) % PLANES), C)
        to_s, e = div(lay, 2), rem(lay, 2)
        mine = rem(to_s, 2) == k
        return mine, (
            back_at(group, copy, pos),
            home_at(e, copy, pos),
            bs.at[group, copy, pos],
            gr.at[pos, e, copy],
            to_s,
            z,
        )

    RB = min(256, dn)

    for pos in reversed(range(pieces)):

        @pl.loop(0, n // 2)
        def _(turn):
            half = rem(turn + c, n // 2)
            q = k * (n // 2) + half
            kind = 0 if pos < 3 else 1 if pos == 3 else 2 if pos < blocks else 3
            left = (xn, xg, x2, xa)[kind]
            left2 = (pxn, pxg, px2, pxa)[kind]
            right, right2 = fulls[kind]
            begin_col = (pos, 0, pos - 4, 0)[kind] * D
            col = slice(begin_col, begin_col + D)
            share = dn if pos < blocks else fn
            block, begin = made_at(pos, q)

            @pl.loop(0, share // RB)
            def _(t):
                mine = left[:, pl.ds(pl.multiple_of(q * share + t * RB, RB), RB)]
                theirs = left2[:, pl.ds(pl.multiple_of(half * share + t * RB, RB), RB)]
                at = pl.ds(pl.multiple_of(begin + t * RB, RB), RB)
                w[block, at, :] = (
                    dot_tokens(mine, right[:, col]) + dot_tokens(theirs, right2[:, col])
                ).astype(BF16)

            start(*relay_copy(pos, half))
            start(*direct_copy(pos, half))

    def total(value):
        return jnp.sum(value, axis=0, keepdims=True)

    dt = jnp.concatenate([total(atp[lag]) for lag in range(lags)], axis=0) * decay[...]
    one, cos1, two, cos2 = (fstate[index] for index in range(4))
    d_tw = dot_tokens(two[:, 0:units], dt, HIGH)
    tw2 = jnp.concatenate([tw[...], jnp.zeros_like(tw)], axis=0)
    d_two = (
        lax.dot_general(dt, tw2, (((1,), (1,)), ((), ())), precision=HIGH, preferred_element_type=F32)
        * cos2
    )
    d_deep = dot_tokens(d_two, one, HIGH)
    d_one = jnp.dot(d_two, ft[:, 128:256], precision=HIGH, preferred_element_type=F32) * cos1
    d_one = jnp.where(lane < units, d_one, 0.0)
    fgrad[:, 0:128] = dot_tokens(d_one, table[...], HIGH)
    fgrad[:, 128:256] = d_deep
    vec = [total(a1[index]) for index in range(7)]
    bias, bias_up = total(abi[...]), total(abu[...])
    taps3 = [total(aks[tap]) for tap in range(3)]
    for q in range(n):
        at = slice(q * dn, (q + 1) * dn)
        for index in range(7):
            sgrad[q, index : index + 1, :] = vec[index][:, at]
        for r in range(3):
            wide_at = slice((3 * q + r) * dn, (3 * q + r + 1) * dn)
            sgrad[q, 7 + r : 8 + r, :] = bias[:, wide_at]
            for tap in range(3):
                row = 10 + 3 * tap + r
                sgrad[q, row : row + 1, :] = taps3[tap][:, wide_at]
        for r in range(wide):
            wide_at = slice((wide * q + r) * dn, (wide * q + r + 1) * dn)
            sgrad[q, 19 + r : 20 + r, :] = bias_up[:, wide_at]
        sgrad[q, SMALL : SMALL + units, :] = d_tw[:, at]

    def vector_copies(q):
        slot = 2 * rho + k
        yield (sgrad.at[q], g_small.at[own_e, slot], vs.at[0, q], vr.at[0, own_e, slot], own_s, q)
        yield (
            fgrad.at[rows(q, un)],
            g_filt.at[own_e, slot],
            vs.at[1, q],
            vr.at[1, own_e, slot],
            own_s,
            q,
        )

    @pl.loop(0, n)
    def _(q):
        for copy in vector_copies(q):
            start(*copy)

    for group in (1, 0):
        for copy in range(R):
            for pos in reversed(range(pieces)):
                mine, args = home_copy(group, copy, pos)

                @pl.when(mine)
                def _():
                    arrived(back_at(group, copy, pos), br.at[group, copy, pos])

                start(*args, mine)

    for copy in token_copies():
        sent(*copy)
    for copy in column_copies():
        sent(*copy)
    for copy in small_copies():
        sent(*copy)
    for group in range(PLANES):
        for pos in range(pieces):
            for copy in plane_copies(group, pos):
                sent(*copy)

    @pl.loop(0, m)
    def _(b):
        @pl.when(jnp.logical_not(last))
        def _():
            for part in range(HOPS):
                hop_forward(b, part).wait_send()

        @pl.when(jnp.logical_not(first))
        def _():
            hop_back(b).wait_send()

        sent(*give_out(b))
        sent(*give_grad(b))

    @pl.loop(0, n)
    def _(q):
        for copy in vector_copies(q):
            sent(*copy)

    @pl.loop(0, n // 2)
    def _(half):
        for pos in range(pieces):
            sent(*relay_copy(pos, half))
            sent(*direct_copy(pos, half))

    for group in range(2):
        for copy in range(R):
            for pos in range(pieces):
                mine, args = home_copy(group, copy, pos)
                sent(*args, mine)

    for core in range(2):
        arrived(r_out.at[rows(jnp.int32(core), MT)], sor.at[core])
        arrived(r_grad.at[rows(jnp.int32(core), MT)], sgr.at[core])

    @pl.loop(0, 2)
    def _(e):
        for slot in range(2 * R):
            arrived(g_small.at[e, slot], vr.at[0, e, slot])
            arrived(g_filt.at[e, slot], vr.at[1, e, slot])
        for copy in range(R):
            for pos in range(pieces):
                arrived(home_at(e, copy, pos), gr.at[pos, e, copy])


def constants(length, width, lags):
    steps = np.arange(lags, dtype=np.float32)
    bands = np.arange(1, 17, dtype=np.float32)
    angles = np.float32(2.0 * np.pi) * steps[:, None] * bands[None, :] / np.float32(length)
    table = np.zeros((lags, 128), np.float32)
    table[:, 0] = steps / length
    table[:, 1:17] = np.cos(angles)
    table[:, 17:33] = np.sin(angles)
    table[:, 33] = 1.0
    rates = np.exp(np.linspace(math.log(0.3), math.log(30.0), width)).astype(np.float32)
    decay = np.exp(-(steps / np.float32(length))[:, None] * rates[None, :]).astype(np.float32)
    return table, decay


def on_device(
    S,
    n,
    tokens,
    cotangent,
    lengths,
    mixer_gain,
    mixer_shift,
    input_weight,
    input_bias,
    short_kernel,
    embed_weight,
    embed_bias,
    filter_weight,
    filter_bias,
    taps_weight,
    skip_gain,
    output_weight,
    output_bias,
    feed_gain,
    feed_shift,
    up_weight,
    up_bias,
    down_weight,
    down_bias,
):
    micro, length, D = tokens.shape
    FF = up_weight.shape[-1]
    dn = mixer_gain.shape[-1]
    units = filter_weight.shape[1]
    un = units // n
    emb = embed_weight.shape[1]
    R = n // PLANES
    m = PLANES
    MT = micro * length // 2
    TT = m * MT
    lags = length // 2
    wide = FF // D

    table, decay = constants(length, D, lags)

    hbm = pl.BlockSpec(memory_space=pl.ANY)
    vmem = pl.BlockSpec(memory_space=pltpu.VMEM)
    smem = pl.BlockSpec(memory_space=pltpu.SMEM)
    dma = pltpu.SemaphoreType.DMA
    blocks = 4 + wide
    pieces = blocks + 1
    out_shape = (
        jax.ShapeDtypeStruct((2, R, dn, 3 * D), BF16),
        jax.ShapeDtypeStruct((2, R, dn, D), BF16),
        jax.ShapeDtypeStruct((2, R, dn, FF), BF16),
        jax.ShapeDtypeStruct((2, R, FF // n, D), BF16),
        jax.ShapeDtypeStruct((2, 2 * R, SMALL + units, dn), F32),
        jax.ShapeDtypeStruct((2, 2 * R, un, 256), F32),
        jax.ShapeDtypeStruct((2 * MT, D), BF16),
        jax.ShapeDtypeStruct((2 * MT, D), BF16),
        jax.ShapeDtypeStruct((PLANES, blocks, dn // 2, D), BF16),
        jax.ShapeDtypeStruct((PLANES, FF // n // 2, D), BF16),
        jax.ShapeDtypeStruct((2, R, blocks, dn, D), BF16),
        jax.ShapeDtypeStruct((2, R, FF // n, D), BF16),
    )
    V = pltpu.VMEM
    scratch = [
        V((blocks + wide, D, D), BF16),
        V((n, SMALL + units, dn), F32),
        V((2 * units, 256), F32),
        V((2, SMALL + units, dn), F32),
        V((2, un, 256), F32),
        V((MT, 128), F32),
        V((128, 128), F32),
        V((8, D), F32),
        V((8, 3 * D), F32),
        V((8, 3 * D), F32),
        V((8, FF), F32),
        V((units, D), F32),
        V((lags, D), F32),
        V((4, lags, 2 * units), F32),
        V((TT, 128), F32),
        V((TT, D), BF16),
        V((TT, D), BF16),
        V((TT, D), BF16),
        V((TT, D), BF16),
        V((TT, D), BF16),
        V((TT, D), BF16),
        V((TT, D), BF16),
        V((TT, FF), BF16),
        V((TT, 3 * D), F32),
        V((TT, 3 * D), F32),
        V((TT, D), F32),
        V((TT, FF), F32),
        V((TT, D), F32),
        V((TT, 3 * D), BF16),
        V((TT, D), BF16),
        V((TT, FF), BF16),
        V((TT, D // 2), BF16),
        V((TT, D // 2), BF16),
        V((TT, D // 2), BF16),
        V((TT, FF // 2), BF16),
        V((TT, 3 * D), BF16),
        V((TT, D), BF16),
        V((TT, FF), BF16),
        V((TT, D), BF16),
        V((7, 8, D), F32),
        V((8, 3 * D), F32),
        V((3, 8, 3 * D), F32),
        V((8, FF), F32),
        V((lags, 8, D), F32),
        V((n, SMALL + units, dn), F32),
        V((2 * units, 256), F32),
        dma((2, 2, pieces)),
        dma((PLANES, pieces)),
        dma((PLANES, R, pieces)),
        dma((pieces, n)),
        dma((pieces, n)),
        dma((pieces, n)),
        dma((2, 2, R, 2)),
        dma((2, n)),
        dma((PLANES,)),
        dma((PLANES,)),
        dma((HOPS,)),
        dma((1,)),
        dma((m, HOPS)),
        dma((m, HOPS)),
        dma((m,)),
        dma((m,)),
        dma((m,)),
        dma((2,)),
        dma((m,)),
        dma((2,)),
        dma((4, m)),
        dma((4, m)),
        dma((4, m)),
        dma((4, m)),
        dma((pieces, n // 2)),
        dma((pieces, 2, R)),
        dma((2, R, pieces)),
        dma((2, R, pieces)),
        dma((2, n)),
        dma((2, 2, 2 * R)),
        pltpu.SemaphoreType.REGULAR,
    ]
    size = (S, n, R, D, FF, m, MT, lags, units, length)
    gi, go, gu, gd, gsm, gft, r_out, r_grad, *_ = pl.pallas_call(
        functools.partial(kernel, size),
        out_shape=out_shape,
        in_specs=[hbm] * 6 + [smem] + [vmem] * 11,
        out_specs=(hbm,) * 12,
        scratch_shapes=scratch,
        compiler_params=pltpu.CompilerParams(
            collective_id=0, has_side_effects=True, vmem_limit_bytes=62 << 20
        ),
        name="window",
    )(
        tokens.reshape(micro * length, D),
        cotangent.reshape(micro * length, D),
        input_weight,
        output_weight,
        up_weight,
        down_weight,
        lengths,
        jnp.stack(
            [mixer_gain, mixer_shift, skip_gain, output_bias, feed_gain, feed_shift, down_bias]
        ),
        input_bias,
        short_kernel,
        up_bias,
        taps_weight,
        embed_weight,
        embed_bias,
        filter_weight,
        filter_bias,
        jnp.asarray(decay),
        jnp.asarray(table),
    )

    def whole(piece):
        return jnp.sum(piece.astype(F32), axis=1)

    vectors = jnp.sum(gsm, axis=1)
    nets = jnp.sum(gft, axis=1)

    def take(begin, count=1):
        return vectors[:, begin : begin + count].reshape(2, count * dn)

    def stream(piece):
        return piece.astype(F32).reshape(1, micro, length, D)

    return (
        stream(r_out),
        stream(r_grad),
        take(0),
        take(1),
        whole(gi),
        take(7, 3),
        vectors[:, 10:19].reshape(2, 3, 3 * dn),
        nets[:, :, 0:emb].transpose(0, 2, 1),
        nets[:, :, emb],
        nets[:, :, 128 : 128 + units].transpose(0, 2, 1),
        nets[:, :, 128 + units],
        vectors[:, SMALL:],
        take(2),
        whole(go),
        take(3),
        take(4),
        take(5),
        whole(gu),
        take(19, wide),
        whole(gd),
        take(6),
    )


def solution(mesh):
    S, n = mesh.shape["section"], mesh.shape["dp"]
    vector, matrix, columns = P("section", "dp"), P("section", "dp", None), P("section", None, "dp")
    weights = (
        vector,
        vector,
        matrix,
        vector,
        columns,
        columns,
        vector,
        columns,
        vector,
        columns,
        vector,
        matrix,
        vector,
        vector,
        vector,
        matrix,
        vector,
        matrix,
        vector,
    )
    rows = P("section", "dp", None, None)
    return jax.shard_map(
        functools.partial(on_device, S, n),
        mesh=mesh,
        in_specs=(P("dp", None, None), P("dp", None, None), P("dp", None)) + weights,
        out_specs=(rows, rows) + weights,
        check_vma=False,
    )
```

```python
import functools
import math

import jax
import jax.numpy as jnp
import numpy as np
from jax import lax
from jax.experimental import pallas as pl
from jax.experimental.pallas import tpu as pltpu
from jax.sharding import PartitionSpec as P

EPSILON = 1e-05
MESH = pl.DeviceIdType.MESH
F32 = jnp.float32
BF16 = jnp.bfloat16
PLANES = 4
SMALL = 32
HIGH = lax.Precision.HIGHEST
HOPS = 2


def div(a, b):
    return lax.div(a, jnp.int32(b))


def rem(a, b):
    return lax.rem(a, jnp.int32(b))


def bits(count):
    return max(0, (count - 1).bit_length())


def gray(p, count):
    if count & (count - 1):
        return p
    return sum(
        (2**b * rem(rem(div(p, 2**b), 2) + rem(div(p, 2 ** (b + 1)), 2), 2) for b in range(bits(count))),
        jnp.int32(0),
    )


def ungray(c, count):
    if count & (count - 1):
        return c
    total = jnp.int32(0)
    for b in range(bits(count)):
        upper = sum((rem(div(c, 2**q), 2) for q in range(b, bits(count))), jnp.int32(0))
        total = total + 2**b * rem(upper, 2)
    return total


def snake(p, group, count):
    back = rem(group, 2)
    return p + back * (count - 1 - 2 * p)


def column_of(layer, columns):
    group = div(layer, columns)
    return gray(snake(rem(layer, columns), group, columns), columns)


def plane_of(layer, columns):
    return rem(div(layer, columns) + 1, PLANES)


def layer_of(column, plane, columns):
    group = rem(plane + PLANES - 1, PLANES)
    return group * columns + snake(ungray(column, columns), group, columns)


def fold(value):
    total = value[0:8]
    for step in range(8, value.shape[0], 8):
        total = total + value[step : step + 8]
    return total


def norm_parts(value):
    centred = value - jnp.mean(value, axis=-1, keepdims=True)
    rate = lax.rsqrt(jnp.mean(centred * centred, axis=-1, keepdims=True) + EPSILON)
    return centred * rate, rate


def norm_back(grad, gain, unit, rate):
    inner = grad * gain
    first = jnp.mean(inner, axis=-1, keepdims=True)
    second = jnp.mean(inner * unit, axis=-1, keepdims=True)
    return rate * (inner - first - unit * second)


def dot_right(left, right):
    return lax.dot_general(left, right, (((1,), (1,)), ((), ())), preferred_element_type=F32)


def dot_rows(left, right):
    count = left.shape[0]
    twice = jnp.concatenate([left, left], axis=0)
    return jnp.dot(twice, right, preferred_element_type=F32)[0:count]


def dot_tokens(left, right, precision=None):
    return lax.dot_general(
        left, right, (((0,), (0,)), ((), ())), precision=precision, preferred_element_type=F32
    )


def kernel(
    size,
    tokens,
    cotangent,
    in_w,
    out_w,
    up_w,
    down_w,
    lengths,
    mixer_gain,
    mixer_shift,
    skip_gain,
    output_bias,
    feed_gain,
    feed_shift,
    down_bias,
    input_bias,
    short_kernel,
    up_bias,
    taps_weight,
    embed_weight,
    embed_bias,
    filter_weight,
    filter_bias,
    decay,
    table,
    g_in_w,
    g_out_w,
    g_up_w,
    g_down_w,
    g_small,
    g_filt,
    r_out,
    r_grad,
    rel,
    rel_down,
    back,
    back_down,
    w,
    sm,
    ft,
    own_sm,
    own_ft,
    own_mask,
    square,
    v1,
    bi,
    ks,
    bu,
    tw,
    taps,
    fstate,
    bm,
    s_in,
    g_arr,
    s_out,
    g_out,
    xn,
    xg,
    x2,
    xa,
    proj,
    conv,
    lcs,
    gpr,
    mid,
    dp,
    dg,
    dh,
    pxn,
    pxg,
    px2,
    pxa,
    pdp,
    pdg,
    pdh,
    pdm,
    a1,
    abi,
    aks,
    abu,
    atp,
    sgrad,
    fgrad,
    ws,
    rr,
    ls,
    wr,
    fs,
    fr,
    ps,
    pr,
    ms,
    mr,
    ts,
    cs,
    hfs,
    hfr,
    hbs,
    hbr,
    sos,
    sor,
    sgs,
    sgr,
    xs,
    xr,
    ds,
    dr,
    gs,
    gr,
    br,
    bs,
    vs,
    vr,
    lag_sem,
):
    S, n, R, D, FF, m, MT, lags, units, length = size
    C = S // 2
    dn, fn, un = D // n, FF // n, units // n
    h, fh = dn // 2, fn // 2
    wide = FF // D
    blocks = 4 + wide
    pieces = blocks + 1
    layers = PLANES * C
    s, z = lax.axis_index("section"), lax.axis_index("dp")
    k, c = rem(s, 2), div(s, 2)
    rho, plane = div(z, PLANES), rem(z, PLANES)
    other = s + 1 - 2 * k
    layer = layer_of(c, plane, C)
    own_s, own_e = div(layer, 2), rem(layer, 2)
    first, last = layer == 0, layer == layers - 1

    def chip_of(stage):
        return 2 * column_of(stage, C) + k, PLANES * rho + plane_of(stage, C)

    next_s, next_z = chip_of(jnp.minimum(layer + 1, layers - 1))
    prev_s, prev_z = chip_of(jnp.maximum(layer - 1, 0))

    def remote(src, dst, send, recv, to_s, to_z):
        return pltpu.make_async_remote_copy(
            src_ref=src,
            dst_ref=dst,
            send_sem=send,
            recv_sem=recv,
            device_id=(to_s, to_z),
            device_id_type=MESH,
        )

    def start(src, dst, send, recv, to_s, to_z, when=True):
        here = jnp.logical_and(to_s == s, to_z == z)

        @pl.when(jnp.logical_and(when, here))
        def _():
            pltpu.make_async_copy(src, dst, recv).start()

        @pl.when(jnp.logical_and(when, jnp.logical_not(here)))
        def _():
            remote(src, dst, send, recv, to_s, to_z).start()

    def sent(src, dst, send, recv, to_s, to_z, when=True):
        here = jnp.logical_and(to_s == s, to_z == z)

        @pl.when(jnp.logical_and(when, jnp.logical_not(here)))
        def _():
            remote(src, dst, send, recv, to_s, to_z).wait_send()

    def arrived(dst, recv):
        remote(dst, dst, recv, recv, other, z).wait_recv()

    def rows(index, count):
        return pl.ds(pl.multiple_of(index * count, count), count)

    barrier = pltpu.get_barrier_semaphore()

    @pl.loop(0, S)
    def _(a):
        @pl.loop(0, n)
        def _(b):
            @pl.when(jnp.logical_or(a != s, b != z))
            def _():
                pl.semaphore_signal(barrier, inc=1, device_id=(a, b), device_id_type=MESH)

    pl.semaphore_wait(barrier, S * n - 1)

    def relay_at(group, pos):
        return rel.at[group, pos] if pos < blocks else rel_down.at[group]

    def held_at(pos, q, core):
        if pos < blocks:
            return w.at[pos, rows(2 * q + core, h)]
        begin = q * fn + core * fh
        return w.at[blocks + div(begin, D), pl.ds(pl.multiple_of(rem(begin, D), fh), fh)]

    def source_at(e, core, pos):
        strip = pl.ds(core * h, h)
        if pos < 3:
            return in_w.at[e, strip, pl.ds(pos * D, D)]
        if pos == 3:
            return out_w.at[e, strip]
        if pos < blocks:
            return up_w.at[e, strip, pl.ds((pos - 4) * D, D)]
        return down_w.at[e, pl.ds(core * fh, fh)]

    def column_copies():
        for pos in range(pieces):
            for e in range(2):
                lay = 2 * s + e
                to_c, group = column_of(lay, C), div(lay, C)
                for core in range(2):
                    yield (
                        source_at(e, core, pos),
                        relay_at(group, pos),
                        ws.at[e, core, pos],
                        rr.at[group, pos],
                        2 * to_c + core,
                        z,
                    )

    def plane_copies(group, pos):
        to_p = (group + 1) % PLANES
        for copy in range(R):
            yield (
                relay_at(group, pos),
                held_at(pos, z, k),
                ls.at[group, copy, pos],
                wr.at[pos, z],
                s,
                PLANES * copy + to_p,
            )

    def pass_on(group, pos):
        arrived(relay_at(group, pos), rr.at[group, pos])
        for copy in plane_copies(group, pos):
            start(*copy)

    first_s, first_z = chip_of(jnp.int32(0))
    last_s, last_z = chip_of(jnp.int32(layers - 1))
    HW = D // HOPS

    def token_copies():
        at = rows(plane, MT)
        for part in range(HOPS):
            col = pl.ds(part * HW, HW)
            yield (
                tokens.at[rows(k, MT), col],
                s_in.at[at, col],
                ts.at[part],
                hfr.at[plane, part],
                first_s,
                first_z,
                s == first_s,
            )
        yield (
            cotangent.at[rows(k, MT)],
            g_arr.at[at],
            cs.at[0],
            hbr.at[plane],
            last_s,
            last_z,
            s == last_s,
        )

    def small_copies():
        for q in range(PLANES):
            yield (own_mask, bm.at[rows(plane, MT)], ms.at[q], mr.at[plane], s, PLANES * rho + q, True)
        for e in range(2):
            lay = 2 * s + e
            to_c, to_p = column_of(lay, C), plane_of(lay, C)
            for copy in range(R):
                to_z = PLANES * copy + to_p
                for core in range(2):
                    to = 2 * to_c + core
                    yield (own_sm.at[e], sm.at[z], ps.at[0, e, copy, core], pr.at[0, z], to, to_z)
                    yield (
                        own_ft.at[e],
                        ft.at[rows(z, un)],
                        ps.at[1, e, copy, core],
                        pr.at[1, z],
                        to,
                        to_z,
                    )

    for copy in token_copies():
        start(*copy)
    for copy in column_copies():
        start(*copy)

    step = lax.broadcasted_iota(jnp.int32, (length, 128), 0)
    for r in range(MT // length):
        begins = step == 0
        begin = jnp.int32(0)
        for doc in range(lengths.shape[1]):
            begin = begin + lengths[k * (MT // length) + r, doc]
            begins = jnp.logical_or(begins, step == begin)
        own_mask[r * length : (r + 1) * length, :] = jnp.where(begins, 0.0, 1.0)

    own_sm[...] = jnp.zeros_like(own_sm)
    shares = (mixer_gain, mixer_shift, skip_gain, output_bias, feed_gain, feed_shift, down_bias)
    for index, share in enumerate(shares):
        own_sm[:, index, :] = share[...].astype(F32)
    wide_bias, wide_up = input_bias[...].astype(F32), up_bias[...].astype(F32)
    for r in range(3):
        own_sm[:, 7 + r, :] = wide_bias[:, r * dn : (r + 1) * dn]
        for e in range(2):
            three = short_kernel[e].astype(F32)
            for tap in range(3):
                own_sm[e, 10 + 3 * tap + r, :] = three[tap, r * dn : (r + 1) * dn]
    for r in range(wide):
        own_sm[:, 19 + r, :] = wide_up[:, r * dn : (r + 1) * dn]
    own_sm[:, SMALL:, :] = taps_weight[...].astype(F32)
    for net, (weight, bias) in enumerate(((embed_weight, embed_bias), (filter_weight, filter_bias))):
        depth = weight.shape[1]
        for e in range(2):
            square[...] = jnp.zeros_like(square)
            square[0:depth, 0:un] = weight[e].astype(F32)
            square[depth : depth + 1, 0:un] = bias[e : e + 1, :].astype(F32)
            own_ft[e, :, net * 128 : (net + 1) * 128] = square[...].T[0:un, :]
    for copy in small_copies():
        start(*copy)

    ft[pl.ds(units, units), :] = jnp.zeros((units, 256), F32)
    a1[...] = jnp.zeros_like(a1)
    abi[...] = jnp.zeros_like(abi)
    aks[...] = jnp.zeros_like(aks)
    abu[...] = jnp.zeros_like(abu)
    atp[...] = jnp.zeros_like(atp)
    sgrad[...] = jnp.zeros_like(sgrad)

    for pos in range(pieces):
        for group in (0, 1):
            pass_on(group, pos)
        for near, group in ((1, 3), (2, 2)):

            @pl.when(plane == near)
            def _():
                pass_on(group, pos)

    defers = layer == C - 1

    def pass_rest():
        for pos in range(pieces):
            for near, group in ((1, 3), (2, 2)):

                @pl.when(plane != near)
                def _():
                    pass_on(group, pos)

    @pl.when(jnp.logical_not(defers))
    def _():
        pass_rest()

    @pl.loop(0, n)
    def _(q):
        arrived(sm.at[q], pr.at[0, q])
        arrived(ft.at[rows(q, un)], pr.at[1, q])

    for q in range(n):
        block = sm[q, 0:SMALL, :]
        v1[:, q * dn : (q + 1) * dn] = block[0:8]
        for r in range(3):
            at = slice((3 * q + r) * dn, (3 * q + r + 1) * dn)
            bi[0:1, at] = block[7 + r : 8 + r]
            for tap in range(3):
                ks[tap : tap + 1, at] = block[10 + 3 * tap + r : 11 + 3 * tap + r]
        for r in range(wide):
            at = slice((wide * q + r) * dn, (wide * q + r + 1) * dn)
            bu[0:1, at] = block[19 + r : 20 + r]
        tw[:, q * dn : (q + 1) * dn] = sm[q, SMALL : SMALL + units, :]

    lane = lax.broadcasted_iota(jnp.int32, (lags, 2 * units), 1)
    embed, deep = ft[:, 0:128], ft[:, 128:256]
    pre1 = lax.dot_general(
        table[...], embed, (((1,), (1,)), ((), ())), precision=HIGH, preferred_element_type=F32
    )
    one = jnp.where(lane == units, 1.0, jnp.sin(pre1))
    pre2 = lax.dot_general(
        one, deep, (((1,), (1,)), ((), ())), precision=HIGH, preferred_element_type=F32
    )
    two = jnp.sin(pre2)
    fstate[0] = one
    fstate[1] = jnp.cos(pre1)
    fstate[2] = two
    fstate[3] = jnp.cos(pre2)
    taps[...] = (
        jnp.dot(two[:, 0:units], tw[...], precision=HIGH, preferred_element_type=F32) * decay[...]
    )

    @pl.loop(0, PLANES)
    def _(q):
        arrived(bm.at[rows(q, MT)], mr.at[q])

    def share_copy(pos, q):
        at = held_at(pos, q, k)
        return remote(at, at, fs.at[pos, q], fr.at[pos, q], other, z)

    @pl.loop(0, n)
    def _(q):
        for pos in range(pieces):
            arrived(held_at(pos, q, k), wr.at[pos, q])
            share_copy(pos, q).start()

    @pl.loop(0, n)
    def _(q):
        for pos in range(pieces):
            share_copy(pos, q).wait()

    CB = 256
    UB = 512
    per = D // UB

    def spread(block, width):
        return jnp.concatenate([block] * (width // 128), axis=1)

    def hop_forward(b, part):
        at, col = rows(b, MT), pl.ds(part * HW, HW)
        return remote(
            s_out.at[at, col], s_in.at[at, col], hfs.at[b, part], hfr.at[b, part], next_s, next_z
        )

    def give_out(b):
        return (
            s_out.at[rows(b, MT)],
            r_out.at[rows(k, MT)],
            sos.at[b],
            sor.at[k],
            own_s,
            PLANES * rho + b,
            own_e == 1,
        )

    def give_grad(b):
        return (
            g_out.at[rows(b, MT)],
            r_grad.at[rows(k, MT)],
            sgs.at[b],
            sgr.at[k],
            own_s,
            PLANES * rho + b,
            own_e == 0,
        )

    halves = ((xn, pxn, D // 2), (xg, pxg, D // 2), (x2, px2, D // 2), (xa, pxa, FF // 2))

    def swap_left(b, pos):
        src, dst, width = halves[pos]
        at = rows(b, MT)
        return remote(
            src.at[at, rows(1 - k, width)], dst.at[at], xs.at[pos, b], xr.at[pos, b], other, z
        )

    fulls = ((dp, pdp), (dg, pdg), (dh, pdh), (g_arr, pdm))

    def swap_right(b, pos):
        src, dst = fulls[pos]
        at = rows(b, MT)
        return remote(src.at[at], dst.at[at], ds.at[pos, b], dr.at[pos, b], other, z)

    @pl.when(jnp.logical_and(first, k == 0))
    def _():
        pl.semaphore_signal(lag_sem, inc=1, device_id=(other, z), device_id_type=MESH)

    @pl.when(jnp.logical_and(first, k == 1))
    def _():
        pl.semaphore_wait(lag_sem, 1)

    @pl.loop(0, m)
    def _(b):
        at = rows(b, MT)
        for part in range(HOPS):
            arrived(s_in.at[at, pl.ds(part * HW, HW)], hfr.at[b, part])
        stream = s_in[at, :].astype(F32)
        unit, _ = norm_parts(stream)
        normed = (unit * v1[0:1, :] + v1[1:2, :]).astype(BF16)
        xn[at, :] = normed
        bb = spread(bm[at, :], CB)
        for cb in range(D // CB):
            col = slice(cb * CB, (cb + 1) * CB)
            parts = []
            for group in range(3):
                wcol = slice(group * D + cb * CB, group * D + (cb + 1) * CB)
                p = dot_rows(normed, w[group, :, col]) + bi[0:1, wcol]
                y1 = bb * pltpu.roll(p, 1, 0)
                y2 = bb * pltpu.roll(y1, 1, 0)
                out = ks[0:1, wcol] * p + ks[1:2, wcol] * y1 + ks[2:3, wcol] * y2
                proj[at, wcol] = p
                conv[at, wcol] = out
                parts.append(out)
            mixed = parts[2] * parts[1]
            total = (v1[2:3, col] + taps[0:1, col]) * mixed
            moved = mixed
            for lag in range(1, lags):
                moved = bb * pltpu.roll(moved, 1, 0)
                total = total + taps[lag : lag + 1, col] * moved
            lcs[at, col] = total
            xg[at, col] = (total * parts[0]).astype(BF16)
        gated = xg[at, :]
        for cb in range(D // CB):
            col = slice(cb * CB, (cb + 1) * CB)
            mid[at, col] = (
                s_in[at, col].astype(F32)
                + dot_rows(gated, w[3, :, col])
                + v1[3:4, col]
            )
        unit, _ = norm_parts(mid[at, :])
        second = (unit * v1[4:5, :] + v1[5:6, :]).astype(BF16)
        x2[at, :] = second
        for ub in range(FF // UB):
            col = slice(ub * UB, (ub + 1) * UB)
            wcol = slice((ub % per) * UB, (ub % per + 1) * UB)
            before = (
                dot_rows(second, w[4 + ub // per, :, wcol]) + bu[0:1, col]
            )
            phi = 0.5 + 0.5 * lax.erf(before * (1.0 / math.sqrt(2.0)))
            dens = jnp.exp(-0.5 * before * before) * (1.0 / math.sqrt(2.0 * math.pi))
            gpr[at, col] = phi + before * dens
            xa[at, col] = (before * phi).astype(BF16)
        for part in range(HOPS):
            col = slice(part * HW, (part + 1) * HW)
            total = mid[at, col] + v1[6:7, col]
            for q in range(wide):
                total = total + dot_rows(xa[at, q * D : (q + 1) * D], w[blocks + q, :, col])
            s_out[at, col] = total.astype(BF16)

            @pl.when(jnp.logical_not(last))
            def _():
                hop_forward(b, part).start()

        start(*give_out(b))
        for pos in range(4):
            swap_left(b, pos).start()

    @pl.when(defers)
    def _():
        pass_rest()

    TB = 256

    @pl.loop(0, blocks + wide)
    def _(b):
        for top in range(D // TB):
            up = slice(top * TB, (top + 1) * TB)
            w[b, up, up] = w[b, up, up].T
            for low in range(top + 1, D // TB):
                down = slice(low * TB, (low + 1) * TB)
                one, two = w[b, up, down], w[b, down, up]
                w[b, up, down] = two.T
                w[b, down, up] = one.T

    def hop_back(b):
        at = rows(b, MT)
        return remote(g_out.at[at], g_arr.at[at], hbs.at[b], hbr.at[b], prev_s, prev_z)

    @pl.when(jnp.logical_and(last, k == 0))
    def _():
        pl.semaphore_signal(lag_sem, inc=1, device_id=(other, z), device_id_type=MESH)

    @pl.when(jnp.logical_and(last, k == 1))
    def _():
        pl.semaphore_wait(lag_sem, 1)

    @pl.loop(0, m)
    def _(b):
        at = rows(b, MT)
        arrived(g_arr.at[at], hbr.at[b])
        swap_right(b, 3).start()
        low = g_arr[at, :]
        grad = low.astype(F32)
        a1[6] += fold(grad)
        for ub in range(FF // UB):
            col = slice(ub * UB, (ub + 1) * UB)
            wcol = slice((ub % per) * UB, (ub % per + 1) * UB)
            inner = (
                dot_rows(low, w[blocks + ub // per, :, wcol])
                * gpr[at, col]
            )
            abu[:, col] += fold(inner)
            dh[at, col] = inner.astype(BF16)
        swap_right(b, 2).start()

        def times(left, begin, count):
            parts = []
            for cb in range(D // CB):
                col = slice(cb * CB, (cb + 1) * CB)
                parts.append(
                    sum(
                        dot_rows(left[at, q * D : (q + 1) * D], w[begin + q, :, col])
                        for q in range(count)
                    )
                )
            return jnp.concatenate(parts, axis=1)

        grad2 = times(dh, 4, wide)
        unit, rate = norm_parts(mid[at, :])
        a1[4] += fold(grad2 * unit)
        a1[5] += fold(grad2)
        middle = grad + norm_back(grad2, v1[4:5, :], unit, rate)
        a1[3] += fold(middle)
        mid[at, :] = middle
        low = middle.astype(BF16)
        dg[at, :] = low
        swap_right(b, 1).start()
        bb = bm[at, :]
        bb = spread(pltpu.roll(bb, MT - 1, 0), CB)
        for cb in range(D // CB):
            col = slice(cb * CB, (cb + 1) * CB)
            gg = dot_rows(low, w[3, :, col])
            cols = [slice(g * D + cb * CB, g * D + (cb + 1) * CB) for g in range(3)]
            c_out, c_in, c_val = (conv[at, item] for item in cols)
            d_out = gg * lcs[at, col]
            moved = gg * c_out
            mixed = c_in * c_val
            direct = fold(moved * mixed)
            a1[2, :, col] += direct
            atp[0, :, col] += direct
            total = (v1[2:3, col] + taps[0:1, col]) * moved
            for lag in range(1, lags):
                moved = bb * pltpu.roll(moved, MT - 1, 0)
                total = total + taps[lag : lag + 1, col] * moved
                atp[lag, :, col] += fold(moved * mixed)
            for item, piece in zip(cols, (d_out, total * c_val, total * c_in)):
                z1 = bb * pltpu.roll(piece, MT - 1, 0)
                z2 = bb * pltpu.roll(z1, MT - 1, 0)
                p = proj[at, item]
                whole = ks[0:1, item] * piece + ks[1:2, item] * z1 + ks[2:3, item] * z2
                aks[0, :, item] += fold(p * piece)
                aks[1, :, item] += fold(p * z1)
                aks[2, :, item] += fold(p * z2)
                abi[:, item] += fold(whole)
                dp[at, item] = whole.astype(BF16)
        swap_right(b, 0).start()
        grad1 = times(dp, 0, 3)
        unit, rate = norm_parts(s_in[at, :].astype(F32))
        a1[0] += fold(grad1 * unit)
        a1[1] += fold(grad1)
        g_out[at, :] = (mid[at, :] + norm_back(grad1, v1[0:1, :], unit, rate)).astype(BF16)

        @pl.when(jnp.logical_not(first))
        def _():
            hop_back(b).start()

        start(*give_grad(b))

    @pl.loop(0, m)
    def _(b):
        for pos in range(4):
            swap_left(b, pos).wait()
            swap_right(b, pos).wait()

    def made_at(pos, q):
        if pos < blocks:
            return pos, q * dn
        return blocks + div(q * fn, D), rem(q * fn, D)

    def home_at(e, copy, pos):
        if pos < 3:
            return g_in_w.at[e, copy, :, pl.ds(pos * D, D)]
        if pos == 3:
            return g_out_w.at[e, copy]
        if pos < blocks:
            return g_up_w.at[e, copy, :, pl.ds((pos - 4) * D, D)]
        return g_down_w.at[e, copy]

    def back_at(group, copy, pos):
        return back.at[group, copy, pos] if pos < blocks else back_down.at[group, copy]

    own_group = div(layer, C)
    relayed = own_group >= 2

    def made(pos, half):
        q = k * (n // 2) + half
        block, begin = made_at(pos, q)
        share = dn if pos < blocks else fn
        return q, w.at[block, pl.ds(pl.multiple_of(begin, share), share)]

    def relay_copy(pos, half):
        q, src = made(pos, half)
        to = jnp.maximum(own_group - 2, 0)
        return (
            src,
            back_at(to, rho, pos),
            gs.at[pos, half],
            br.at[to, rho, pos],
            2 * c + rem(own_s, 2),
            q,
            relayed,
        )

    def direct_copy(pos, half):
        q, src = made(pos, half)
        return (
            src,
            home_at(own_e, rho, pos),
            gs.at[pos, half],
            gr.at[pos, own_e, rho],
            own_s,
            q,
            jnp.logical_not(relayed),
        )

    def home_copy(group, copy, pos):
        lay = layer_of(c, jnp.int32((group + 3) % PLANES), C)
        to_s, e = div(lay, 2), rem(lay, 2)
        mine = rem(to_s, 2) == k
        return mine, (
            back_at(group, copy, pos),
            home_at(e, copy, pos),
            bs.at[group, copy, pos],
            gr.at[pos, e, copy],
            to_s,
            z,
        )

    RB = min(256, dn)

    for pos in reversed(range(pieces)):

        @pl.loop(0, n // 2)
        def _(turn):
            half = rem(turn + c, n // 2)
            q = k * (n // 2) + half
            kind = 0 if pos < 3 else 1 if pos == 3 else 2 if pos < blocks else 3
            left = (xn, xg, x2, xa)[kind]
            left2 = (pxn, pxg, px2, pxa)[kind]
            right, right2 = fulls[kind]
            begin_col = (pos, 0, pos - 4, 0)[kind] * D
            col = slice(begin_col, begin_col + D)
            share = dn if pos < blocks else fn
            block, begin = made_at(pos, q)

            @pl.loop(0, share // RB)
            def _(t):
                mine = left[:, pl.ds(pl.multiple_of(q * share + t * RB, RB), RB)]
                theirs = left2[:, pl.ds(pl.multiple_of(half * share + t * RB, RB), RB)]
                at = pl.ds(pl.multiple_of(begin + t * RB, RB), RB)
                w[block, at, :] = (
                    dot_tokens(mine, right[:, col]) + dot_tokens(theirs, right2[:, col])
                ).astype(BF16)

            start(*relay_copy(pos, half))
            start(*direct_copy(pos, half))

    def total(value):
        return jnp.sum(value, axis=0, keepdims=True)

    dt = jnp.concatenate([total(atp[lag]) for lag in range(lags)], axis=0) * decay[...]
    one, cos1, two, cos2 = (fstate[index] for index in range(4))
    d_tw = dot_tokens(two[:, 0:units], dt, HIGH)
    tw2 = jnp.concatenate([tw[...], jnp.zeros_like(tw)], axis=0)
    d_two = (
        lax.dot_general(dt, tw2, (((1,), (1,)), ((), ())), precision=HIGH, preferred_element_type=F32)
        * cos2
    )
    d_deep = dot_tokens(d_two, one, HIGH)
    d_one = jnp.dot(d_two, ft[:, 128:256], precision=HIGH, preferred_element_type=F32) * cos1
    d_one = jnp.where(lane < units, d_one, 0.0)
    fgrad[:, 0:128] = dot_tokens(d_one, table[...], HIGH)
    fgrad[:, 128:256] = d_deep
    vec = [total(a1[index]) for index in range(7)]
    bias, bias_up = total(abi[...]), total(abu[...])
    taps3 = [total(aks[tap]) for tap in range(3)]
    for q in range(n):
        at = slice(q * dn, (q + 1) * dn)
        for index in range(7):
            sgrad[q, index : index + 1, :] = vec[index][:, at]
        for r in range(3):
            wide_at = slice((3 * q + r) * dn, (3 * q + r + 1) * dn)
            sgrad[q, 7 + r : 8 + r, :] = bias[:, wide_at]
            for tap in range(3):
                row = 10 + 3 * tap + r
                sgrad[q, row : row + 1, :] = taps3[tap][:, wide_at]
        for r in range(wide):
            wide_at = slice((wide * q + r) * dn, (wide * q + r + 1) * dn)
            sgrad[q, 19 + r : 20 + r, :] = bias_up[:, wide_at]
        sgrad[q, SMALL : SMALL + units, :] = d_tw[:, at]

    def vector_copies(q):
        slot = 2 * rho + k
        yield (sgrad.at[q], g_small.at[own_e, slot], vs.at[0, q], vr.at[0, own_e, slot], own_s, q)
        yield (
            fgrad.at[rows(q, un)],
            g_filt.at[own_e, slot],
            vs.at[1, q],
            vr.at[1, own_e, slot],
            own_s,
            q,
        )

    @pl.loop(0, n)
    def _(q):
        for copy in vector_copies(q):
            start(*copy)

    for group in (1, 0):
        for copy in range(R):
            for pos in reversed(range(pieces)):
                mine, args = home_copy(group, copy, pos)

                @pl.when(mine)
                def _():
                    arrived(back_at(group, copy, pos), br.at[group, copy, pos])

                start(*args, mine)

    for copy in token_copies():
        sent(*copy)
    for copy in column_copies():
        sent(*copy)
    for copy in small_copies():
        sent(*copy)
    for group in range(PLANES):
        for pos in range(pieces):
            for copy in plane_copies(group, pos):
                sent(*copy)

    @pl.loop(0, m)
    def _(b):
        @pl.when(jnp.logical_not(last))
        def _():
            for part in range(HOPS):
                hop_forward(b, part).wait_send()

        @pl.when(jnp.logical_not(first))
        def _():
            hop_back(b).wait_send()

        sent(*give_out(b))
        sent(*give_grad(b))

    @pl.loop(0, n)
    def _(q):
        for copy in vector_copies(q):
            sent(*copy)

    @pl.loop(0, n // 2)
    def _(half):
        for pos in range(pieces):
            sent(*relay_copy(pos, half))
            sent(*direct_copy(pos, half))

    for group in range(2):
        for copy in range(R):
            for pos in range(pieces):
                mine, args = home_copy(group, copy, pos)
                sent(*args, mine)

    for core in range(2):
        arrived(r_out.at[rows(jnp.int32(core), MT)], sor.at[core])
        arrived(r_grad.at[rows(jnp.int32(core), MT)], sgr.at[core])

    @pl.loop(0, 2)
    def _(e):
        for slot in range(2 * R):
            arrived(g_small.at[e, slot], vr.at[0, e, slot])
            arrived(g_filt.at[e, slot], vr.at[1, e, slot])
        for copy in range(R):
            for pos in range(pieces):
                arrived(home_at(e, copy, pos), gr.at[pos, e, copy])


def constants(length, width, lags):
    steps = np.arange(lags, dtype=np.float32)
    bands = np.arange(1, 17, dtype=np.float32)
    angles = np.float32(2.0 * np.pi) * steps[:, None] * bands[None, :] / np.float32(length)
    table = np.zeros((lags, 128), np.float32)
    table[:, 0] = steps / length
    table[:, 1:17] = np.cos(angles)
    table[:, 17:33] = np.sin(angles)
    table[:, 33] = 1.0
    rates = np.exp(np.linspace(math.log(0.3), math.log(30.0), width)).astype(np.float32)
    decay = np.exp(-(steps / np.float32(length))[:, None] * rates[None, :]).astype(np.float32)
    return table, decay


def on_device(
    S,
    n,
    tokens,
    cotangent,
    lengths,
    mixer_gain,
    mixer_shift,
    input_weight,
    input_bias,
    short_kernel,
    embed_weight,
    embed_bias,
    filter_weight,
    filter_bias,
    taps_weight,
    skip_gain,
    output_weight,
    output_bias,
    feed_gain,
    feed_shift,
    up_weight,
    up_bias,
    down_weight,
    down_bias,
):
    micro, length, D = tokens.shape
    FF = up_weight.shape[-1]
    dn = mixer_gain.shape[-1]
    units = filter_weight.shape[1]
    un = units // n
    emb = embed_weight.shape[1]
    R = n // PLANES
    m = PLANES
    MT = micro * length // 2
    TT = m * MT
    lags = length // 2
    wide = FF // D

    table, decay = constants(length, D, lags)

    hbm = pl.BlockSpec(memory_space=pl.ANY)
    vmem = pl.BlockSpec(memory_space=pltpu.VMEM)
    smem = pl.BlockSpec(memory_space=pltpu.SMEM)
    dma = pltpu.SemaphoreType.DMA
    blocks = 4 + wide
    pieces = blocks + 1
    out_shape = (
        jax.ShapeDtypeStruct((2, R, dn, 3 * D), BF16),
        jax.ShapeDtypeStruct((2, R, dn, D), BF16),
        jax.ShapeDtypeStruct((2, R, dn, FF), BF16),
        jax.ShapeDtypeStruct((2, R, FF // n, D), BF16),
        jax.ShapeDtypeStruct((2, 2 * R, SMALL + units, dn), F32),
        jax.ShapeDtypeStruct((2, 2 * R, un, 256), F32),
        jax.ShapeDtypeStruct((2 * MT, D), BF16),
        jax.ShapeDtypeStruct((2 * MT, D), BF16),
        jax.ShapeDtypeStruct((PLANES, blocks, dn // 2, D), BF16),
        jax.ShapeDtypeStruct((PLANES, FF // n // 2, D), BF16),
        jax.ShapeDtypeStruct((2, R, blocks, dn, D), BF16),
        jax.ShapeDtypeStruct((2, R, FF // n, D), BF16),
    )
    V = pltpu.VMEM
    scratch = [
        V((blocks + wide, D, D), BF16),
        V((n, SMALL + units, dn), F32),
        V((2 * units, 256), F32),
        V((2, SMALL + units, dn), F32),
        V((2, un, 256), F32),
        V((MT, 128), F32),
        V((128, 128), F32),
        V((8, D), F32),
        V((8, 3 * D), F32),
        V((8, 3 * D), F32),
        V((8, FF), F32),
        V((units, D), F32),
        V((lags, D), F32),
        V((4, lags, 2 * units), F32),
        V((TT, 128), F32),
        V((TT, D), BF16),
        V((TT, D), BF16),
        V((TT, D), BF16),
        V((TT, D), BF16),
        V((TT, D), BF16),
        V((TT, D), BF16),
        V((TT, D), BF16),
        V((TT, FF), BF16),
        V((TT, 3 * D), F32),
        V((TT, 3 * D), F32),
        V((TT, D), F32),
        V((TT, FF), F32),
        V((TT, D), F32),
        V((TT, 3 * D), BF16),
        V((TT, D), BF16),
        V((TT, FF), BF16),
        V((TT, D // 2), BF16),
        V((TT, D // 2), BF16),
        V((TT, D // 2), BF16),
        V((TT, FF // 2), BF16),
        V((TT, 3 * D), BF16),
        V((TT, D), BF16),
        V((TT, FF), BF16),
        V((TT, D), BF16),
        V((7, 8, D), F32),
        V((8, 3 * D), F32),
        V((3, 8, 3 * D), F32),
        V((8, FF), F32),
        V((lags, 8, D), F32),
        V((n, SMALL + units, dn), F32),
        V((2 * units, 256), F32),
        dma((2, 2, pieces)),
        dma((PLANES, pieces)),
        dma((PLANES, R, pieces)),
        dma((pieces, n)),
        dma((pieces, n)),
        dma((pieces, n)),
        dma((2, 2, R, 2)),
        dma((2, n)),
        dma((PLANES,)),
        dma((PLANES,)),
        dma((HOPS,)),
        dma((1,)),
        dma((m, HOPS)),
        dma((m, HOPS)),
        dma((m,)),
        dma((m,)),
        dma((m,)),
        dma((2,)),
        dma((m,)),
        dma((2,)),
        dma((4, m)),
        dma((4, m)),
        dma((4, m)),
        dma((4, m)),
        dma((pieces, n // 2)),
        dma((pieces, 2, R)),
        dma((2, R, pieces)),
        dma((2, R, pieces)),
        dma((2, n)),
        dma((2, 2, 2 * R)),
        pltpu.SemaphoreType.REGULAR,
    ]
    size = (S, n, R, D, FF, m, MT, lags, units, length)
    gi, go, gu, gd, gsm, gft, r_out, r_grad, *_ = pl.pallas_call(
        functools.partial(kernel, size),
        out_shape=out_shape,
        in_specs=[hbm] * 6 + [smem] + [vmem] * 17,
        out_specs=(hbm,) * 12,
        scratch_shapes=scratch,
        compiler_params=pltpu.CompilerParams(
            collective_id=0, has_side_effects=True, vmem_limit_bytes=62 << 20
        ),
        name="window",
    )(
        tokens.reshape(micro * length, D),
        cotangent.reshape(micro * length, D),
        input_weight,
        output_weight,
        up_weight,
        down_weight,
        lengths,
        mixer_gain,
        mixer_shift,
        skip_gain,
        output_bias,
        feed_gain,
        feed_shift,
        down_bias,
        input_bias,
        short_kernel,
        up_bias,
        taps_weight,
        embed_weight,
        embed_bias,
        filter_weight,
        filter_bias,
        jnp.asarray(decay),
        jnp.asarray(table),
    )

    def whole(piece):
        return jnp.sum(piece.astype(F32), axis=1)

    vectors = jnp.sum(gsm, axis=1)
    nets = jnp.sum(gft, axis=1)

    def take(begin, count=1):
        return vectors[:, begin : begin + count].reshape(2, count * dn)

    def stream(piece):
        return piece.astype(F32).reshape(1, micro, length, D)

    return (
        stream(r_out),
        stream(r_grad),
        take(0),
        take(1),
        whole(gi),
        take(7, 3),
        vectors[:, 10:19].reshape(2, 3, 3 * dn),
        nets[:, :, 0:emb].transpose(0, 2, 1),
        nets[:, :, emb],
        nets[:, :, 128 : 128 + units].transpose(0, 2, 1),
        nets[:, :, 128 + units],
        vectors[:, SMALL:],
        take(2),
        whole(go),
        take(3),
        take(4),
        take(5),
        whole(gu),
        take(19, wide),
        whole(gd),
        take(6),
    )


def solution(mesh):
    S, n = mesh.shape["section"], mesh.shape["dp"]
    vector, matrix, columns = P("section", "dp"), P("section", "dp", None), P("section", None, "dp")
    weights = (
        vector,
        vector,
        matrix,
        vector,
        columns,
        columns,
        vector,
        columns,
        vector,
        columns,
        vector,
        matrix,
        vector,
        vector,
        vector,
        matrix,
        vector,
        matrix,
        vector,
    )
    rows = P("section", "dp", None, None)
    return jax.shard_map(
        functools.partial(on_device, S, n),
        mesh=mesh,
        in_specs=(P("dp", None, None), P("dp", None, None), P("dp", None)) + weights,
        out_specs=(rows, rows) + weights,
        check_vma=False,
    )
```

```python
import functools
import math

import jax
import jax.numpy as jnp
import numpy as np
from jax import lax
from jax.experimental import pallas as pl
from jax.experimental.pallas import tpu as pltpu
from jax.sharding import PartitionSpec as P

EPSILON = 1e-05
MESH = pl.DeviceIdType.MESH
F32 = jnp.float32
BF16 = jnp.bfloat16
PLANES = 4
SMALL = 32
HIGH = lax.Precision.HIGHEST
HOPS = 2


def div(a, b):
    return lax.div(a, jnp.int32(b))


def rem(a, b):
    return lax.rem(a, jnp.int32(b))


def bits(count):
    return max(0, (count - 1).bit_length())


def gray(p, count):
    if count & (count - 1):
        return p
    return sum(
        (2**b * rem(rem(div(p, 2**b), 2) + rem(div(p, 2 ** (b + 1)), 2), 2) for b in range(bits(count))),
        jnp.int32(0),
    )


def ungray(c, count):
    if count & (count - 1):
        return c
    total = jnp.int32(0)
    for b in range(bits(count)):
        upper = sum((rem(div(c, 2**q), 2) for q in range(b, bits(count))), jnp.int32(0))
        total = total + 2**b * rem(upper, 2)
    return total


def snake(p, group, count):
    back = rem(group, 2)
    return p + back * (count - 1 - 2 * p)


def column_of(layer, columns):
    group = div(layer, columns)
    return gray(snake(rem(layer, columns), group, columns), columns)


def plane_of(layer, columns):
    return rem(div(layer, columns) + 1, PLANES)


def layer_of(column, plane, columns):
    group = rem(plane + PLANES - 1, PLANES)
    return group * columns + snake(ungray(column, columns), group, columns)


def fold(value):
    total = value[0:8]
    for step in range(8, value.shape[0], 8):
        total = total + value[step : step + 8]
    return total


def norm_parts(value):
    centred = value - jnp.mean(value, axis=-1, keepdims=True)
    rate = lax.rsqrt(jnp.mean(centred * centred, axis=-1, keepdims=True) + EPSILON)
    return centred * rate, rate


def norm_back(grad, gain, unit, rate):
    inner = grad * gain
    first = jnp.mean(inner, axis=-1, keepdims=True)
    second = jnp.mean(inner * unit, axis=-1, keepdims=True)
    return rate * (inner - first - unit * second)


def dot_right(left, right):
    return lax.dot_general(left, right, (((1,), (1,)), ((), ())), preferred_element_type=F32)


def dot_rows(left, right):
    count = left.shape[0]
    twice = jnp.concatenate([left, left], axis=0)
    return jnp.dot(twice, right, preferred_element_type=F32)[0:count]


def dot_tokens(left, right, precision=None):
    return lax.dot_general(
        left, right, (((0,), (0,)), ((), ())), precision=precision, preferred_element_type=F32
    )


def kernel(
    size,
    tokens,
    cotangent,
    in_w,
    out_w,
    up_w,
    down_w,
    lengths,
    mixer_gain,
    mixer_shift,
    skip_gain,
    output_bias,
    feed_gain,
    feed_shift,
    down_bias,
    input_bias,
    short_kernel,
    up_bias,
    taps_weight,
    embed_weight,
    embed_bias,
    filter_weight,
    filter_bias,
    decay,
    table,
    g_in_w,
    g_out_w,
    g_up_w,
    g_down_w,
    g_small,
    g_filt,
    r_out,
    r_grad,
    rel,
    rel_down,
    back,
    back_down,
    w,
    sm,
    ft,
    own_sm,
    own_ft,
    own_mask,
    square,
    v1,
    bi,
    ks,
    bu,
    tw,
    taps,
    fstate,
    bm,
    s_in,
    g_arr,
    s_out,
    g_out,
    xn,
    xg,
    x2,
    xa,
    proj,
    conv,
    lcs,
    gpr,
    mid,
    dp,
    dg,
    dh,
    pxn,
    pxg,
    px2,
    pxa,
    pdp,
    pdg,
    pdh,
    pdm,
    a1,
    abi,
    aks,
    abu,
    atp,
    sgrad,
    fgrad,
    ws,
    rr,
    ls,
    wr,
    fs,
    fr,
    ps,
    pr,
    ms,
    mr,
    ts,
    cs,
    hfs,
    hfr,
    hbs,
    hbr,
    sos,
    sor,
    sgs,
    sgr,
    xs,
    xr,
    ds,
    dr,
    gs,
    gr,
    br,
    bs,
    vs,
    vr,
    lag_sem,
):
    S, n, R, D, FF, m, MT, lags, units, length = size
    C = S // 2
    dn, fn, un = D // n, FF // n, units // n
    h, fh = dn // 2, fn // 2
    wide = FF // D
    blocks = 4 + wide
    pieces = blocks + 1
    layers = PLANES * C
    s, z = lax.axis_index("section"), lax.axis_index("dp")
    k, c = rem(s, 2), div(s, 2)
    rho, plane = div(z, PLANES), rem(z, PLANES)
    other = s + 1 - 2 * k
    layer = layer_of(c, plane, C)
    own_s, own_e = div(layer, 2), rem(layer, 2)
    first, last = layer == 0, layer == layers - 1

    def chip_of(stage):
        return 2 * column_of(stage, C) + k, PLANES * rho + plane_of(stage, C)

    next_s, next_z = chip_of(jnp.minimum(layer + 1, layers - 1))
    prev_s, prev_z = chip_of(jnp.maximum(layer - 1, 0))

    def remote(src, dst, send, recv, to_s, to_z):
        return pltpu.make_async_remote_copy(
            src_ref=src,
            dst_ref=dst,
            send_sem=send,
            recv_sem=recv,
            device_id=(to_s, to_z),
            device_id_type=MESH,
        )

    def start(src, dst, send, recv, to_s, to_z, when=True):
        here = jnp.logical_and(to_s == s, to_z == z)

        @pl.when(jnp.logical_and(when, here))
        def _():
            pltpu.make_async_copy(src, dst, recv).start()

        @pl.when(jnp.logical_and(when, jnp.logical_not(here)))
        def _():
            remote(src, dst, send, recv, to_s, to_z).start()

    def sent(src, dst, send, recv, to_s, to_z, when=True):
        here = jnp.logical_and(to_s == s, to_z == z)

        @pl.when(jnp.logical_and(when, jnp.logical_not(here)))
        def _():
            remote(src, dst, send, recv, to_s, to_z).wait_send()

    def arrived(dst, recv):
        remote(dst, dst, recv, recv, other, z).wait_recv()

    def rows(index, count):
        return pl.ds(pl.multiple_of(index * count, count), count)

    barrier = pltpu.get_barrier_semaphore()

    @pl.loop(0, S)
    def _(a):
        @pl.loop(0, n)
        def _(b):
            @pl.when(jnp.logical_or(a != s, b != z))
            def _():
                pl.semaphore_signal(barrier, inc=1, device_id=(a, b), device_id_type=MESH)

    pl.semaphore_wait(barrier, S * n - 1)

    def relay_at(group, pos):
        return rel.at[group, pos] if pos < blocks else rel_down.at[group]

    def held_at(pos, q, core):
        if pos < blocks:
            return w.at[pos, rows(2 * q + core, h)]
        begin = q * fn + core * fh
        return w.at[blocks + div(begin, D), pl.ds(pl.multiple_of(rem(begin, D), fh), fh)]

    def source_at(e, core, pos):
        strip = pl.ds(core * h, h)
        if pos < 3:
            return in_w.at[e, strip, pl.ds(pos * D, D)]
        if pos == 3:
            return out_w.at[e, strip]
        if pos < blocks:
            return up_w.at[e, strip, pl.ds((pos - 4) * D, D)]
        return down_w.at[e, pl.ds(core * fh, fh)]

    def column_copies():
        for pos in range(pieces):
            for e in range(2):
                lay = 2 * s + e
                to_c, group = column_of(lay, C), div(lay, C)
                for core in range(2):
                    yield (
                        source_at(e, core, pos),
                        relay_at(group, pos),
                        ws.at[e, core, pos],
                        rr.at[group, pos],
                        2 * to_c + core,
                        z,
                    )

    def plane_copies(group, pos):
        to_p = (group + 1) % PLANES
        for copy in range(R):
            yield (
                relay_at(group, pos),
                held_at(pos, z, k),
                ls.at[group, copy, pos],
                wr.at[pos, z],
                s,
                PLANES * copy + to_p,
            )

    def pass_on(group, pos):
        arrived(relay_at(group, pos), rr.at[group, pos])
        for copy in plane_copies(group, pos):
            start(*copy)

    first_s, first_z = chip_of(jnp.int32(0))
    last_s, last_z = chip_of(jnp.int32(layers - 1))
    HW = D // HOPS

    def token_copies():
        at = rows(plane, MT)
        for part in range(HOPS):
            col = pl.ds(part * HW, HW)
            yield (
                tokens.at[rows(k, MT), col],
                s_in.at[at, col],
                ts.at[part],
                hfr.at[plane, part],
                first_s,
                first_z,
                s == first_s,
            )
        yield (
            cotangent.at[rows(k, MT)],
            g_arr.at[at],
            cs.at[0],
            hbr.at[plane],
            last_s,
            last_z,
            s == last_s,
        )

    def small_copies():
        for q in range(PLANES):
            yield (own_mask, bm.at[rows(plane, MT)], ms.at[q], mr.at[plane], s, PLANES * rho + q, True)
        for e in range(2):
            lay = 2 * s + e
            to_c, to_p = column_of(lay, C), plane_of(lay, C)
            for copy in range(R):
                to_z = PLANES * copy + to_p
                for core in range(2):
                    to = 2 * to_c + core
                    yield (own_sm.at[e], sm.at[z], ps.at[0, e, copy, core], pr.at[0, z], to, to_z)
                    yield (
                        own_ft.at[e],
                        ft.at[rows(z, un)],
                        ps.at[1, e, copy, core],
                        pr.at[1, z],
                        to,
                        to_z,
                    )

    for copy in token_copies():
        start(*copy)
    for copy in column_copies():
        start(*copy)

    step = lax.broadcasted_iota(jnp.int32, (length, 128), 0)
    for r in range(MT // length):
        begins = step == 0
        begin = jnp.int32(0)
        for doc in range(lengths.shape[1]):
            begin = begin + lengths[k * (MT // length) + r, doc]
            begins = jnp.logical_or(begins, step == begin)
        own_mask[r * length : (r + 1) * length, :] = jnp.where(begins, 0.0, 1.0)

    own_sm[...] = jnp.zeros_like(own_sm)
    shares = (mixer_gain, mixer_shift, skip_gain, output_bias, feed_gain, feed_shift, down_bias)
    for index, share in enumerate(shares):
        own_sm[:, index, :] = share[...].astype(F32)
    wide_bias, wide_up = input_bias[...].astype(F32), up_bias[...].astype(F32)
    for r in range(3):
        own_sm[:, 7 + r, :] = wide_bias[:, r * dn : (r + 1) * dn]
        for e in range(2):
            three = short_kernel[e].astype(F32)
            for tap in range(3):
                own_sm[e, 10 + 3 * tap + r, :] = three[tap, r * dn : (r + 1) * dn]
    for r in range(wide):
        own_sm[:, 19 + r, :] = wide_up[:, r * dn : (r + 1) * dn]
    own_sm[:, SMALL:, :] = taps_weight[...].astype(F32)
    for net, (weight, bias) in enumerate(((embed_weight, embed_bias), (filter_weight, filter_bias))):
        depth = weight.shape[1]
        for e in range(2):
            square[...] = jnp.zeros_like(square)
            square[0:depth, 0:un] = weight[e].astype(F32)
            square[depth : depth + 1, 0:un] = bias[e : e + 1, :].astype(F32)
            own_ft[e, :, net * 128 : (net + 1) * 128] = square[...].T[0:un, :]
    for copy in small_copies():
        start(*copy)

    ft[pl.ds(units, units), :] = jnp.zeros((units, 256), F32)
    a1[...] = jnp.zeros_like(a1)
    abi[...] = jnp.zeros_like(abi)
    aks[...] = jnp.zeros_like(aks)
    abu[...] = jnp.zeros_like(abu)
    atp[...] = jnp.zeros_like(atp)
    sgrad[...] = jnp.zeros_like(sgrad)

    for pos in range(pieces):
        for group in (0, 1):
            pass_on(group, pos)
        for near, group in ((1, 3), (2, 2)):

            @pl.when(plane == near)
            def _():
                pass_on(group, pos)

    for pos in range(pieces):
        for near, group in ((1, 3), (2, 2)):

            @pl.when(plane != near)
            def _():
                pass_on(group, pos)

    @pl.loop(0, n)
    def _(q):
        arrived(sm.at[q], pr.at[0, q])
        arrived(ft.at[rows(q, un)], pr.at[1, q])

    for q in range(n):
        block = sm[q, 0:SMALL, :]
        v1[:, q * dn : (q + 1) * dn] = block[0:8]
        for r in range(3):
            at = slice((3 * q + r) * dn, (3 * q + r + 1) * dn)
            bi[0:1, at] = block[7 + r : 8 + r]
            for tap in range(3):
                ks[tap : tap + 1, at] = block[10 + 3 * tap + r : 11 + 3 * tap + r]
        for r in range(wide):
            at = slice((wide * q + r) * dn, (wide * q + r + 1) * dn)
            bu[0:1, at] = block[19 + r : 20 + r]
        tw[:, q * dn : (q + 1) * dn] = sm[q, SMALL : SMALL + units, :]

    lane = lax.broadcasted_iota(jnp.int32, (lags, 2 * units), 1)
    embed, deep = ft[:, 0:128], ft[:, 128:256]
    pre1 = lax.dot_general(
        table[...], embed, (((1,), (1,)), ((), ())), precision=HIGH, preferred_element_type=F32
    )
    one = jnp.where(lane == units, 1.0, jnp.sin(pre1))
    pre2 = lax.dot_general(
        one, deep, (((1,), (1,)), ((), ())), precision=HIGH, preferred_element_type=F32
    )
    two = jnp.sin(pre2)
    fstate[0] = one
    fstate[1] = jnp.cos(pre1)
    fstate[2] = two
    fstate[3] = jnp.cos(pre2)
    taps[...] = (
        jnp.dot(two[:, 0:units], tw[...], precision=HIGH, preferred_element_type=F32) * decay[...]
    )

    @pl.loop(0, PLANES)
    def _(q):
        arrived(bm.at[rows(q, MT)], mr.at[q])

    def share_copy(pos, q):
        at = held_at(pos, q, k)
        return remote(at, at, fs.at[pos, q], fr.at[pos, q], other, z)

    @pl.loop(0, n)
    def _(q):
        for pos in range(pieces):
            arrived(held_at(pos, q, k), wr.at[pos, q])
            share_copy(pos, q).start()

    @pl.loop(0, n)
    def _(q):
        for pos in range(pieces):
            share_copy(pos, q).wait()

    CB = 256
    UB = 512
    per = D // UB

    def spread(block, width):
        return jnp.concatenate([block] * (width // 128), axis=1)

    def hop_forward(b, part):
        at, col = rows(b, MT), pl.ds(part * HW, HW)
        return remote(
            s_out.at[at, col], s_in.at[at, col], hfs.at[b, part], hfr.at[b, part], next_s, next_z
        )

    def give_out(b):
        return (
            s_out.at[rows(b, MT)],
            r_out.at[rows(k, MT)],
            sos.at[b],
            sor.at[k],
            own_s,
            PLANES * rho + b,
            own_e == 1,
        )

    def give_grad(b):
        return (
            g_out.at[rows(b, MT)],
            r_grad.at[rows(k, MT)],
            sgs.at[b],
            sgr.at[k],
            own_s,
            PLANES * rho + b,
            own_e == 0,
        )

    halves = ((xn, pxn, D // 2), (xg, pxg, D // 2), (x2, px2, D // 2), (xa, pxa, FF // 2))

    def swap_left(b, pos):
        src, dst, width = halves[pos]
        at = rows(b, MT)
        return remote(
            src.at[at, rows(1 - k, width)], dst.at[at], xs.at[pos, b], xr.at[pos, b], other, z
        )

    fulls = ((dp, pdp), (dg, pdg), (dh, pdh), (g_arr, pdm))

    def swap_right(b, pos):
        src, dst = fulls[pos]
        at = rows(b, MT)
        return remote(src.at[at], dst.at[at], ds.at[pos, b], dr.at[pos, b], other, z)

    @pl.when(jnp.logical_and(first, k == 0))
    def _():
        pl.semaphore_signal(lag_sem, inc=1, device_id=(other, z), device_id_type=MESH)

    @pl.when(jnp.logical_and(first, k == 1))
    def _():
        pl.semaphore_wait(lag_sem, 1)

    @pl.loop(0, m)
    def _(b):
        at = rows(b, MT)
        for part in range(HOPS):
            arrived(s_in.at[at, pl.ds(part * HW, HW)], hfr.at[b, part])
        stream = s_in[at, :].astype(F32)
        unit, _ = norm_parts(stream)
        normed = (unit * v1[0:1, :] + v1[1:2, :]).astype(BF16)
        xn[at, :] = normed
        bb = spread(bm[at, :], CB)
        for cb in range(D // CB):
            col = slice(cb * CB, (cb + 1) * CB)
            parts = []
            for group in range(3):
                wcol = slice(group * D + cb * CB, group * D + (cb + 1) * CB)
                p = dot_rows(normed, w[group, :, col]) + bi[0:1, wcol]
                y1 = bb * pltpu.roll(p, 1, 0)
                y2 = bb * pltpu.roll(y1, 1, 0)
                out = ks[0:1, wcol] * p + ks[1:2, wcol] * y1 + ks[2:3, wcol] * y2
                proj[at, wcol] = p
                conv[at, wcol] = out
                parts.append(out)
            mixed = parts[2] * parts[1]
            total = (v1[2:3, col] + taps[0:1, col]) * mixed
            moved = mixed
            for lag in range(1, lags):
                moved = bb * pltpu.roll(moved, 1, 0)
                total = total + taps[lag : lag + 1, col] * moved
            lcs[at, col] = total
            xg[at, col] = (total * parts[0]).astype(BF16)
        gated = xg[at, :]
        for cb in range(D // CB):
            col = slice(cb * CB, (cb + 1) * CB)
            mid[at, col] = (
                s_in[at, col].astype(F32)
                + dot_rows(gated, w[3, :, col])
                + v1[3:4, col]
            )
        unit, _ = norm_parts(mid[at, :])
        second = (unit * v1[4:5, :] + v1[5:6, :]).astype(BF16)
        x2[at, :] = second
        for ub in range(FF // UB):
            col = slice(ub * UB, (ub + 1) * UB)
            wcol = slice((ub % per) * UB, (ub % per + 1) * UB)
            before = (
                dot_rows(second, w[4 + ub // per, :, wcol]) + bu[0:1, col]
            )
            phi = 0.5 + 0.5 * lax.erf(before * (1.0 / math.sqrt(2.0)))
            dens = jnp.exp(-0.5 * before * before) * (1.0 / math.sqrt(2.0 * math.pi))
            gpr[at, col] = phi + before * dens
            xa[at, col] = (before * phi).astype(BF16)
        for part in range(HOPS):
            col = slice(part * HW, (part + 1) * HW)
            total = mid[at, col] + v1[6:7, col]
            for q in range(wide):
                total = total + dot_rows(xa[at, q * D : (q + 1) * D], w[blocks + q, :, col])
            s_out[at, col] = total.astype(BF16)

            @pl.when(jnp.logical_not(last))
            def _():
                hop_forward(b, part).start()

        start(*give_out(b))
        for pos in range(4):
            swap_left(b, pos).start()

    TB = 256

    @pl.loop(0, blocks + wide)
    def _(b):
        for top in range(D // TB):
            up = slice(top * TB, (top + 1) * TB)
            w[b, up, up] = w[b, up, up].T
            for low in range(top + 1, D // TB):
                down = slice(low * TB, (low + 1) * TB)
                one, two = w[b, up, down], w[b, down, up]
                w[b, up, down] = two.T
                w[b, down, up] = one.T

    def hop_back(b):
        at = rows(b, MT)
        return remote(g_out.at[at], g_arr.at[at], hbs.at[b], hbr.at[b], prev_s, prev_z)

    @pl.when(jnp.logical_and(last, k == 0))
    def _():
        pl.semaphore_signal(lag_sem, inc=1, device_id=(other, z), device_id_type=MESH)

    @pl.when(jnp.logical_and(last, k == 1))
    def _():
        pl.semaphore_wait(lag_sem, 1)

    @pl.loop(0, m)
    def _(b):
        at = rows(b, MT)
        arrived(g_arr.at[at], hbr.at[b])
        swap_right(b, 3).start()
        low = g_arr[at, :]
        grad = low.astype(F32)
        a1[6] += fold(grad)
        for ub in range(FF // UB):
            col = slice(ub * UB, (ub + 1) * UB)
            wcol = slice((ub % per) * UB, (ub % per + 1) * UB)
            inner = (
                dot_rows(low, w[blocks + ub // per, :, wcol])
                * gpr[at, col]
            )
            abu[:, col] += fold(inner)
            dh[at, col] = inner.astype(BF16)
        swap_right(b, 2).start()

        def times(left, begin, count):
            parts = []
            for cb in range(D // CB):
                col = slice(cb * CB, (cb + 1) * CB)
                parts.append(
                    sum(
                        dot_rows(left[at, q * D : (q + 1) * D], w[begin + q, :, col])
                        for q in range(count)
                    )
                )
            return jnp.concatenate(parts, axis=1)

        grad2 = times(dh, 4, wide)
        unit, rate = norm_parts(mid[at, :])
        a1[4] += fold(grad2 * unit)
        a1[5] += fold(grad2)
        middle = grad + norm_back(grad2, v1[4:5, :], unit, rate)
        a1[3] += fold(middle)
        mid[at, :] = middle
        low = middle.astype(BF16)
        dg[at, :] = low
        swap_right(b, 1).start()
        bb = bm[at, :]
        bb = spread(pltpu.roll(bb, MT - 1, 0), CB)
        for cb in range(D // CB):
            col = slice(cb * CB, (cb + 1) * CB)
            gg = dot_rows(low, w[3, :, col])
            cols = [slice(g * D + cb * CB, g * D + (cb + 1) * CB) for g in range(3)]
            c_out, c_in, c_val = (conv[at, item] for item in cols)
            d_out = gg * lcs[at, col]
            moved = gg * c_out
            mixed = c_in * c_val
            direct = fold(moved * mixed)
            a1[2, :, col] += direct
            atp[0, :, col] += direct
            total = (v1[2:3, col] + taps[0:1, col]) * moved
            for lag in range(1, lags):
                moved = bb * pltpu.roll(moved, MT - 1, 0)
                total = total + taps[lag : lag + 1, col] * moved
                atp[lag, :, col] += fold(moved * mixed)
            for item, piece in zip(cols, (d_out, total * c_val, total * c_in)):
                z1 = bb * pltpu.roll(piece, MT - 1, 0)
                z2 = bb * pltpu.roll(z1, MT - 1, 0)
                p = proj[at, item]
                whole = ks[0:1, item] * piece + ks[1:2, item] * z1 + ks[2:3, item] * z2
                aks[0, :, item] += fold(p * piece)
                aks[1, :, item] += fold(p * z1)
                aks[2, :, item] += fold(p * z2)
                abi[:, item] += fold(whole)
                dp[at, item] = whole.astype(BF16)
        swap_right(b, 0).start()
        grad1 = times(dp, 0, 3)
        unit, rate = norm_parts(s_in[at, :].astype(F32))
        a1[0] += fold(grad1 * unit)
        a1[1] += fold(grad1)
        g_out[at, :] = (mid[at, :] + norm_back(grad1, v1[0:1, :], unit, rate)).astype(BF16)

        @pl.when(jnp.logical_not(first))
        def _():
            hop_back(b).start()

        start(*give_grad(b))

    @pl.loop(0, m)
    def _(b):
        for pos in range(4):
            swap_left(b, pos).wait()
            swap_right(b, pos).wait()

    def made_at(pos, q):
        if pos < blocks:
            return pos, q * dn
        return blocks + div(q * fn, D), rem(q * fn, D)

    def home_at(e, copy, pos):
        if pos < 3:
            return g_in_w.at[e, copy, :, pl.ds(pos * D, D)]
        if pos == 3:
            return g_out_w.at[e, copy]
        if pos < blocks:
            return g_up_w.at[e, copy, :, pl.ds((pos - 4) * D, D)]
        return g_down_w.at[e, copy]

    def back_at(group, copy, pos):
        return back.at[group, copy, pos] if pos < blocks else back_down.at[group, copy]

    own_group = div(layer, C)
    relayed = own_group >= 2

    def made(pos, half):
        q = k * (n // 2) + half
        block, begin = made_at(pos, q)
        share = dn if pos < blocks else fn
        return q, w.at[block, pl.ds(pl.multiple_of(begin, share), share)]

    def relay_copy(pos, half):
        q, src = made(pos, half)
        to = jnp.maximum(own_group - 2, 0)
        return (
            src,
            back_at(to, rho, pos),
            gs.at[pos, half],
            br.at[to, rho, pos],
            2 * c + rem(own_s, 2),
            q,
            relayed,
        )

    def direct_copy(pos, half):
        q, src = made(pos, half)
        return (
            src,
            home_at(own_e, rho, pos),
            gs.at[pos, half],
            gr.at[pos, own_e, rho],
            own_s,
            q,
            jnp.logical_not(relayed),
        )

    def home_copy(group, copy, pos):
        lay = layer_of(c, jnp.int32((group + 3) % PLANES), C)
        to_s, e = div(lay, 2), rem(lay, 2)
        mine = rem(to_s, 2) == k
        return mine, (
            back_at(group, copy, pos),
            home_at(e, copy, pos),
            bs.at[group, copy, pos],
            gr.at[pos, e, copy],
            to_s,
            z,
        )

    RB = min(256, dn)

    for pos in reversed(range(pieces)):

        @pl.loop(0, n // 2)
        def _(turn):
            half = rem(turn + c, n // 2)
            q = k * (n // 2) + half
            kind = 0 if pos < 3 else 1 if pos == 3 else 2 if pos < blocks else 3
            left = (xn, xg, x2, xa)[kind]
            left2 = (pxn, pxg, px2, pxa)[kind]
            right, right2 = fulls[kind]
            begin_col = (pos, 0, pos - 4, 0)[kind] * D
            col = slice(begin_col, begin_col + D)
            share = dn if pos < blocks else fn
            block, begin = made_at(pos, q)

            @pl.loop(0, share // RB)
            def _(t):
                mine = left[:, pl.ds(pl.multiple_of(q * share + t * RB, RB), RB)]
                theirs = left2[:, pl.ds(pl.multiple_of(half * share + t * RB, RB), RB)]
                at = pl.ds(pl.multiple_of(begin + t * RB, RB), RB)
                w[block, at, :] = (
                    dot_tokens(mine, right[:, col]) + dot_tokens(theirs, right2[:, col])
                ).astype(BF16)

            start(*relay_copy(pos, half))
            start(*direct_copy(pos, half))

    def total(value):
        return jnp.sum(value, axis=0, keepdims=True)

    dt = jnp.concatenate([total(atp[lag]) for lag in range(lags)], axis=0) * decay[...]
    one, cos1, two, cos2 = (fstate[index] for index in range(4))
    d_tw = dot_tokens(two[:, 0:units], dt, HIGH)
    tw2 = jnp.concatenate([tw[...], jnp.zeros_like(tw)], axis=0)
    d_two = (
        lax.dot_general(dt, tw2, (((1,), (1,)), ((), ())), precision=HIGH, preferred_element_type=F32)
        * cos2
    )
    d_deep = dot_tokens(d_two, one, HIGH)
    d_one = jnp.dot(d_two, ft[:, 128:256], precision=HIGH, preferred_element_type=F32) * cos1
    d_one = jnp.where(lane < units, d_one, 0.0)
    fgrad[:, 0:128] = dot_tokens(d_one, table[...], HIGH)
    fgrad[:, 128:256] = d_deep
    vec = [total(a1[index]) for index in range(7)]
    bias, bias_up = total(abi[...]), total(abu[...])
    taps3 = [total(aks[tap]) for tap in range(3)]
    for q in range(n):
        at = slice(q * dn, (q + 1) * dn)
        for index in range(7):
            sgrad[q, index : index + 1, :] = vec[index][:, at]
        for r in range(3):
            wide_at = slice((3 * q + r) * dn, (3 * q + r + 1) * dn)
            sgrad[q, 7 + r : 8 + r, :] = bias[:, wide_at]
            for tap in range(3):
                row = 10 + 3 * tap + r
                sgrad[q, row : row + 1, :] = taps3[tap][:, wide_at]
        for r in range(wide):
            wide_at = slice((wide * q + r) * dn, (wide * q + r + 1) * dn)
            sgrad[q, 19 + r : 20 + r, :] = bias_up[:, wide_at]
        sgrad[q, SMALL : SMALL + units, :] = d_tw[:, at]

    def vector_copies(q):
        slot = 2 * rho + k
        yield (sgrad.at[q], g_small.at[own_e, slot], vs.at[0, q], vr.at[0, own_e, slot], own_s, q)
        yield (
            fgrad.at[rows(q, un)],
            g_filt.at[own_e, slot],
            vs.at[1, q],
            vr.at[1, own_e, slot],
            own_s,
            q,
        )

    @pl.loop(0, n)
    def _(q):
        for copy in vector_copies(q):
            start(*copy)

    for group in (1, 0):
        for copy in range(R):
            for pos in reversed(range(pieces)):
                mine, args = home_copy(group, copy, pos)

                @pl.when(mine)
                def _():
                    arrived(back_at(group, copy, pos), br.at[group, copy, pos])

                start(*args, mine)

    for copy in token_copies():
        sent(*copy)
    for copy in column_copies():
        sent(*copy)
    for copy in small_copies():
        sent(*copy)
    for group in range(PLANES):
        for pos in range(pieces):
            for copy in plane_copies(group, pos):
                sent(*copy)

    @pl.loop(0, m)
    def _(b):
        @pl.when(jnp.logical_not(last))
        def _():
            for part in range(HOPS):
                hop_forward(b, part).wait_send()

        @pl.when(jnp.logical_not(first))
        def _():
            hop_back(b).wait_send()

        sent(*give_out(b))
        sent(*give_grad(b))

    @pl.loop(0, n)
    def _(q):
        for copy in vector_copies(q):
            sent(*copy)

    @pl.loop(0, n // 2)
    def _(half):
        for pos in range(pieces):
            sent(*relay_copy(pos, half))
            sent(*direct_copy(pos, half))

    for group in range(2):
        for copy in range(R):
            for pos in range(pieces):
                mine, args = home_copy(group, copy, pos)
                sent(*args, mine)

    for core in range(2):
        arrived(r_out.at[rows(jnp.int32(core), MT)], sor.at[core])
        arrived(r_grad.at[rows(jnp.int32(core), MT)], sgr.at[core])

    @pl.loop(0, 2)
    def _(e):
        for slot in range(2 * R):
            arrived(g_small.at[e, slot], vr.at[0, e, slot])
            arrived(g_filt.at[e, slot], vr.at[1, e, slot])
        for copy in range(R):
            for pos in range(pieces):
                arrived(home_at(e, copy, pos), gr.at[pos, e, copy])


def constants(length, width, lags):
    steps = np.arange(lags, dtype=np.float32)
    bands = np.arange(1, 17, dtype=np.float32)
    angles = np.float32(2.0 * np.pi) * steps[:, None] * bands[None, :] / np.float32(length)
    table = np.zeros((lags, 128), np.float32)
    table[:, 0] = steps / length
    table[:, 1:17] = np.cos(angles)
    table[:, 17:33] = np.sin(angles)
    table[:, 33] = 1.0
    rates = np.exp(np.linspace(math.log(0.3), math.log(30.0), width)).astype(np.float32)
    decay = np.exp(-(steps / np.float32(length))[:, None] * rates[None, :]).astype(np.float32)
    return table, decay


def on_device(
    S,
    n,
    tokens,
    cotangent,
    lengths,
    mixer_gain,
    mixer_shift,
    input_weight,
    input_bias,
    short_kernel,
    embed_weight,
    embed_bias,
    filter_weight,
    filter_bias,
    taps_weight,
    skip_gain,
    output_weight,
    output_bias,
    feed_gain,
    feed_shift,
    up_weight,
    up_bias,
    down_weight,
    down_bias,
):
    micro, length, D = tokens.shape
    FF = up_weight.shape[-1]
    dn = mixer_gain.shape[-1]
    units = filter_weight.shape[1]
    un = units // n
    emb = embed_weight.shape[1]
    R = n // PLANES
    m = PLANES
    MT = micro * length // 2
    TT = m * MT
    lags = length // 2
    wide = FF // D

    table, decay = constants(length, D, lags)

    hbm = pl.BlockSpec(memory_space=pl.ANY)
    vmem = pl.BlockSpec(memory_space=pltpu.VMEM)
    smem = pl.BlockSpec(memory_space=pltpu.SMEM)
    dma = pltpu.SemaphoreType.DMA
    blocks = 4 + wide
    pieces = blocks + 1
    out_shape = (
        jax.ShapeDtypeStruct((2, R, dn, 3 * D), BF16),
        jax.ShapeDtypeStruct((2, R, dn, D), BF16),
        jax.ShapeDtypeStruct((2, R, dn, FF), BF16),
        jax.ShapeDtypeStruct((2, R, FF // n, D), BF16),
        jax.ShapeDtypeStruct((2, 2 * R, SMALL + units, dn), F32),
        jax.ShapeDtypeStruct((2, 2 * R, un, 256), F32),
        jax.ShapeDtypeStruct((2 * MT, D), BF16),
        jax.ShapeDtypeStruct((2 * MT, D), BF16),
        jax.ShapeDtypeStruct((PLANES, blocks, dn // 2, D), BF16),
        jax.ShapeDtypeStruct((PLANES, FF // n // 2, D), BF16),
        jax.ShapeDtypeStruct((2, R, blocks, dn, D), BF16),
        jax.ShapeDtypeStruct((2, R, FF // n, D), BF16),
    )
    V = pltpu.VMEM
    scratch = [
        V((blocks + wide, D, D), BF16),
        V((n, SMALL + units, dn), F32),
        V((2 * units, 256), F32),
        V((2, SMALL + units, dn), F32),
        V((2, un, 256), F32),
        V((MT, 128), F32),
        V((128, 128), F32),
        V((8, D), F32),
        V((8, 3 * D), F32),
        V((8, 3 * D), F32),
        V((8, FF), F32),
        V((units, D), F32),
        V((lags, D), F32),
        V((4, lags, 2 * units), F32),
        V((TT, 128), F32),
        V((TT, D), BF16),
        V((TT, D), BF16),
        V((TT, D), BF16),
        V((TT, D), BF16),
        V((TT, D), BF16),
        V((TT, D), BF16),
        V((TT, D), BF16),
        V((TT, FF), BF16),
        V((TT, 3 * D), F32),
        V((TT, 3 * D), F32),
        V((TT, D), F32),
        V((TT, FF), F32),
        V((TT, D), F32),
        V((TT, 3 * D), BF16),
        V((TT, D), BF16),
        V((TT, FF), BF16),
        V((TT, D // 2), BF16),
        V((TT, D // 2), BF16),
        V((TT, D // 2), BF16),
        V((TT, FF // 2), BF16),
        V((TT, 3 * D), BF16),
        V((TT, D), BF16),
        V((TT, FF), BF16),
        V((TT, D), BF16),
        V((7, 8, D), F32),
        V((8, 3 * D), F32),
        V((3, 8, 3 * D), F32),
        V((8, FF), F32),
        V((lags, 8, D), F32),
        V((n, SMALL + units, dn), F32),
        V((2 * units, 256), F32),
        dma((2, 2, pieces)),
        dma((PLANES, pieces)),
        dma((PLANES, R, pieces)),
        dma((pieces, n)),
        dma((pieces, n)),
        dma((pieces, n)),
        dma((2, 2, R, 2)),
        dma((2, n)),
        dma((PLANES,)),
        dma((PLANES,)),
        dma((HOPS,)),
        dma((1,)),
        dma((m, HOPS)),
        dma((m, HOPS)),
        dma((m,)),
        dma((m,)),
        dma((m,)),
        dma((2,)),
        dma((m,)),
        dma((2,)),
        dma((4, m)),
        dma((4, m)),
        dma((4, m)),
        dma((4, m)),
        dma((pieces, n // 2)),
        dma((pieces, 2, R)),
        dma((2, R, pieces)),
        dma((2, R, pieces)),
        dma((2, n)),
        dma((2, 2, 2 * R)),
        pltpu.SemaphoreType.REGULAR,
    ]
    size = (S, n, R, D, FF, m, MT, lags, units, length)
    gi, go, gu, gd, gsm, gft, r_out, r_grad, *_ = pl.pallas_call(
        functools.partial(kernel, size),
        out_shape=out_shape,
        in_specs=[hbm] * 6 + [smem] + [vmem] * 17,
        out_specs=(hbm,) * 12,
        scratch_shapes=scratch,
        compiler_params=pltpu.CompilerParams(
            collective_id=0, has_side_effects=True, vmem_limit_bytes=62 << 20
        ),
        name="window",
    )(
        tokens.reshape(micro * length, D),
        cotangent.reshape(micro * length, D),
        input_weight,
        output_weight,
        up_weight,
        down_weight,
        lengths,
        mixer_gain,
        mixer_shift,
        skip_gain,
        output_bias,
        feed_gain,
        feed_shift,
        down_bias,
        input_bias,
        short_kernel,
        up_bias,
        taps_weight,
        embed_weight,
        embed_bias,
        filter_weight,
        filter_bias,
        jnp.asarray(decay),
        jnp.asarray(table),
    )

    def whole(piece):
        return jnp.sum(piece.astype(F32), axis=1)

    vectors = jnp.sum(gsm, axis=1)
    nets = jnp.sum(gft, axis=1)

    def take(begin, count=1):
        return vectors[:, begin : begin + count].reshape(2, count * dn)

    def stream(piece):
        return piece.astype(F32).reshape(1, micro, length, D)

    return (
        stream(r_out),
        stream(r_grad),
        take(0),
        take(1),
        whole(gi),
        take(7, 3),
        vectors[:, 10:19].reshape(2, 3, 3 * dn),
        nets[:, :, 0:emb].transpose(0, 2, 1),
        nets[:, :, emb],
        nets[:, :, 128 : 128 + units].transpose(0, 2, 1),
        nets[:, :, 128 + units],
        vectors[:, SMALL:],
        take(2),
        whole(go),
        take(3),
        take(4),
        take(5),
        whole(gu),
        take(19, wide),
        whole(gd),
        take(6),
    )


def solution(mesh):
    S, n = mesh.shape["section"], mesh.shape["dp"]
    vector, matrix, columns = P("section", "dp"), P("section", "dp", None), P("section", None, "dp")
    weights = (
        vector,
        vector,
        matrix,
        vector,
        columns,
        columns,
        vector,
        columns,
        vector,
        columns,
        vector,
        matrix,
        vector,
        vector,
        vector,
        matrix,
        vector,
        matrix,
        vector,
    )
    rows = P("section", "dp", None, None)
    return jax.shard_map(
        functools.partial(on_device, S, n),
        mesh=mesh,
        in_specs=(P("dp", None, None), P("dp", None, None), P("dp", None)) + weights,
        out_specs=(rows, rows) + weights,
        check_vma=False,
    )
```

```python
import functools
import math

import jax
import jax.numpy as jnp
import numpy as np
from jax import lax
from jax.experimental import pallas as pl
from jax.experimental.pallas import tpu as pltpu
from jax.sharding import PartitionSpec as P

EPSILON = 1e-05
MESH = pl.DeviceIdType.MESH
F32 = jnp.float32
BF16 = jnp.bfloat16
PLANES = 4
SMALL = 32
HIGH = lax.Precision.HIGHEST
HOPS = 2


def div(a, b):
    return lax.div(a, jnp.int32(b))


def rem(a, b):
    return lax.rem(a, jnp.int32(b))


def bits(count):
    return max(0, (count - 1).bit_length())


def gray(p, count):
    if count & (count - 1):
        return p
    return sum(
        (2**b * rem(rem(div(p, 2**b), 2) + rem(div(p, 2 ** (b + 1)), 2), 2) for b in range(bits(count))),
        jnp.int32(0),
    )


def ungray(c, count):
    if count & (count - 1):
        return c
    total = jnp.int32(0)
    for b in range(bits(count)):
        upper = sum((rem(div(c, 2**q), 2) for q in range(b, bits(count))), jnp.int32(0))
        total = total + 2**b * rem(upper, 2)
    return total


def snake(p, group, count):
    back = rem(group, 2)
    return p + back * (count - 1 - 2 * p)


def column_of(layer, columns):
    group = div(layer, columns)
    return gray(snake(rem(layer, columns), group, columns), columns)


def plane_of(layer, columns):
    return rem(div(layer, columns) + 1, PLANES)


def layer_of(column, plane, columns):
    group = rem(plane + PLANES - 1, PLANES)
    return group * columns + snake(ungray(column, columns), group, columns)


def fold(value):
    total = value[0:8]
    for step in range(8, value.shape[0], 8):
        total = total + value[step : step + 8]
    return total


def norm_parts(value):
    centred = value - jnp.mean(value, axis=-1, keepdims=True)
    rate = lax.rsqrt(jnp.mean(centred * centred, axis=-1, keepdims=True) + EPSILON)
    return centred * rate, rate


def norm_back(grad, gain, unit, rate):
    inner = grad * gain
    first = jnp.mean(inner, axis=-1, keepdims=True)
    second = jnp.mean(inner * unit, axis=-1, keepdims=True)
    return rate * (inner - first - unit * second)


def dot_right(left, right):
    return lax.dot_general(left, right, (((1,), (1,)), ((), ())), preferred_element_type=F32)


def dot_rows(left, right):
    count = left.shape[0]
    twice = jnp.concatenate([left, left], axis=0)
    return jnp.dot(twice, right, preferred_element_type=F32)[0:count]


def dot_tokens(left, right, precision=None):
    return lax.dot_general(
        left, right, (((0,), (0,)), ((), ())), precision=precision, preferred_element_type=F32
    )


def kernel(
    size,
    tokens,
    cotangent,
    in_w,
    out_w,
    up_w,
    down_w,
    lengths,
    mixer_gain,
    mixer_shift,
    skip_gain,
    output_bias,
    feed_gain,
    feed_shift,
    down_bias,
    input_bias,
    short_kernel,
    up_bias,
    taps_weight,
    embed_weight,
    embed_bias,
    filter_weight,
    filter_bias,
    decay,
    table,
    g_in_w,
    g_out_w,
    g_up_w,
    g_down_w,
    g_small,
    g_filt,
    r_out,
    r_grad,
    rel,
    rel_down,
    back,
    back_down,
    w,
    sm,
    ft,
    own_sm,
    own_ft,
    own_mask,
    square,
    v1,
    bi,
    ks,
    bu,
    tw,
    taps,
    fstate,
    bm,
    s_in,
    g_arr,
    s_out,
    g_out,
    xn,
    xg,
    x2,
    xa,
    proj,
    conv,
    lcs,
    gpr,
    mid,
    dp,
    dg,
    dh,
    pxn,
    pxg,
    px2,
    pxa,
    pdp,
    pdg,
    pdh,
    pdm,
    a1,
    abi,
    aks,
    abu,
    atp,
    sgrad,
    fgrad,
    ws,
    rr,
    ls,
    wr,
    fs,
    fr,
    ps,
    pr,
    ms,
    mr,
    ts,
    cs,
    hfs,
    hfr,
    hbs,
    hbr,
    sos,
    sor,
    sgs,
    sgr,
    xs,
    xr,
    ds,
    dr,
    gs,
    gr,
    br,
    bs,
    vs,
    vr,
    lag_sem,
):
    S, n, R, D, FF, m, MT, lags, units, length = size
    C = S // 2
    dn, fn, un = D // n, FF // n, units // n
    h, fh = dn // 2, fn // 2
    wide = FF // D
    blocks = 4 + wide
    pieces = blocks + 1
    order = (blocks,) + tuple(range(blocks))
    layers = PLANES * C
    s, z = lax.axis_index("section"), lax.axis_index("dp")
    k, c = rem(s, 2), div(s, 2)
    rho, plane = div(z, PLANES), rem(z, PLANES)
    other = s + 1 - 2 * k
    layer = layer_of(c, plane, C)
    own_s, own_e = div(layer, 2), rem(layer, 2)
    first, last = layer == 0, layer == layers - 1

    def chip_of(stage):
        return 2 * column_of(stage, C) + k, PLANES * rho + plane_of(stage, C)

    next_s, next_z = chip_of(jnp.minimum(layer + 1, layers - 1))
    prev_s, prev_z = chip_of(jnp.maximum(layer - 1, 0))

    def remote(src, dst, send, recv, to_s, to_z):
        return pltpu.make_async_remote_copy(
            src_ref=src,
            dst_ref=dst,
            send_sem=send,
            recv_sem=recv,
            device_id=(to_s, to_z),
            device_id_type=MESH,
        )

    def start(src, dst, send, recv, to_s, to_z, when=True):
        here = jnp.logical_and(to_s == s, to_z == z)

        @pl.when(jnp.logical_and(when, here))
        def _():
            pltpu.make_async_copy(src, dst, recv).start()

        @pl.when(jnp.logical_and(when, jnp.logical_not(here)))
        def _():
            remote(src, dst, send, recv, to_s, to_z).start()

    def sent(src, dst, send, recv, to_s, to_z, when=True):
        here = jnp.logical_and(to_s == s, to_z == z)

        @pl.when(jnp.logical_and(when, jnp.logical_not(here)))
        def _():
            remote(src, dst, send, recv, to_s, to_z).wait_send()

    def arrived(dst, recv):
        remote(dst, dst, recv, recv, other, z).wait_recv()

    def rows(index, count):
        return pl.ds(pl.multiple_of(index * count, count), count)

    barrier = pltpu.get_barrier_semaphore()

    @pl.loop(0, S)
    def _(a):
        @pl.loop(0, n)
        def _(b):
            @pl.when(jnp.logical_or(a != s, b != z))
            def _():
                pl.semaphore_signal(barrier, inc=1, device_id=(a, b), device_id_type=MESH)

    pl.semaphore_wait(barrier, S * n - 1)

    def relay_at(group, pos):
        return rel.at[group, pos] if pos < blocks else rel_down.at[group]

    def held_at(pos, q, core):
        if pos < blocks:
            return w.at[pos, rows(2 * q + core, h)]
        begin = q * fn + core * fh
        return w.at[blocks + div(begin, D), pl.ds(pl.multiple_of(rem(begin, D), fh), fh)]

    def source_at(e, core, pos):
        strip = pl.ds(core * h, h)
        if pos < 3:
            return in_w.at[e, strip, pl.ds(pos * D, D)]
        if pos == 3:
            return out_w.at[e, strip]
        if pos < blocks:
            return up_w.at[e, strip, pl.ds((pos - 4) * D, D)]
        return down_w.at[e, pl.ds(core * fh, fh)]

    def column_copies():
        for pos in order:
            for e in range(2):
                lay = 2 * s + e
                to_c, group = column_of(lay, C), div(lay, C)
                for core in range(2):
                    yield (
                        source_at(e, core, pos),
                        relay_at(group, pos),
                        ws.at[e, core, pos],
                        rr.at[group, pos],
                        2 * to_c + core,
                        z,
                    )

    def plane_copies(group, pos):
        to_p = (group + 1) % PLANES
        for copy in range(R):
            yield (
                relay_at(group, pos),
                held_at(pos, z, k),
                ls.at[group, copy, pos],
                wr.at[pos, z],
                s,
                PLANES * copy + to_p,
            )

    def pass_on(group, pos):
        arrived(relay_at(group, pos), rr.at[group, pos])
        for copy in plane_copies(group, pos):
            start(*copy)

    first_s, first_z = chip_of(jnp.int32(0))
    last_s, last_z = chip_of(jnp.int32(layers - 1))
    HW = D // HOPS

    def token_copies():
        at = rows(plane, MT)
        for part in range(HOPS):
            col = pl.ds(part * HW, HW)
            yield (
                tokens.at[rows(k, MT), col],
                s_in.at[at, col],
                ts.at[part],
                hfr.at[plane, part],
                first_s,
                first_z,
                s == first_s,
            )
        yield (
            cotangent.at[rows(k, MT)],
            g_arr.at[at],
            cs.at[0],
            hbr.at[plane],
            last_s,
            last_z,
            s == last_s,
        )

    def small_copies():
        for q in range(PLANES):
            yield (own_mask, bm.at[rows(plane, MT)], ms.at[q], mr.at[plane], s, PLANES * rho + q, True)
        for e in range(2):
            lay = 2 * s + e
            to_c, to_p = column_of(lay, C), plane_of(lay, C)
            for copy in range(R):
                to_z = PLANES * copy + to_p
                for core in range(2):
                    to = 2 * to_c + core
                    yield (own_sm.at[e], sm.at[z], ps.at[0, e, copy, core], pr.at[0, z], to, to_z)
                    yield (
                        own_ft.at[e],
                        ft.at[rows(z, un)],
                        ps.at[1, e, copy, core],
                        pr.at[1, z],
                        to,
                        to_z,
                    )

    for copy in token_copies():
        start(*copy)
    for copy in column_copies():
        start(*copy)

    step = lax.broadcasted_iota(jnp.int32, (length, 128), 0)
    for r in range(MT // length):
        begins = step == 0
        begin = jnp.int32(0)
        for doc in range(lengths.shape[1]):
            begin = begin + lengths[k * (MT // length) + r, doc]
            begins = jnp.logical_or(begins, step == begin)
        own_mask[r * length : (r + 1) * length, :] = jnp.where(begins, 0.0, 1.0)

    own_sm[...] = jnp.zeros_like(own_sm)
    shares = (mixer_gain, mixer_shift, skip_gain, output_bias, feed_gain, feed_shift, down_bias)
    for index, share in enumerate(shares):
        own_sm[:, index, :] = share[...].astype(F32)
    wide_bias, wide_up = input_bias[...].astype(F32), up_bias[...].astype(F32)
    for r in range(3):
        own_sm[:, 7 + r, :] = wide_bias[:, r * dn : (r + 1) * dn]
        for e in range(2):
            three = short_kernel[e].astype(F32)
            for tap in range(3):
                own_sm[e, 10 + 3 * tap + r, :] = three[tap, r * dn : (r + 1) * dn]
    for r in range(wide):
        own_sm[:, 19 + r, :] = wide_up[:, r * dn : (r + 1) * dn]
    own_sm[:, SMALL:, :] = taps_weight[...].astype(F32)
    for net, (weight, bias) in enumerate(((embed_weight, embed_bias), (filter_weight, filter_bias))):
        depth = weight.shape[1]
        for e in range(2):
            square[...] = jnp.zeros_like(square)
            square[0:depth, 0:un] = weight[e].astype(F32)
            square[depth : depth + 1, 0:un] = bias[e : e + 1, :].astype(F32)
            own_ft[e, :, net * 128 : (net + 1) * 128] = square[...].T[0:un, :]
    for copy in small_copies():
        start(*copy)

    ft[pl.ds(units, units), :] = jnp.zeros((units, 256), F32)
    a1[...] = jnp.zeros_like(a1)
    abi[...] = jnp.zeros_like(abi)
    aks[...] = jnp.zeros_like(aks)
    abu[...] = jnp.zeros_like(abu)
    atp[...] = jnp.zeros_like(atp)
    sgrad[...] = jnp.zeros_like(sgrad)

    for pos in order:
        for group in (0, 1):
            pass_on(group, pos)
        for near, group in ((1, 3), (2, 2)):

            @pl.when(plane == near)
            def _():
                pass_on(group, pos)

    for pos in order:
        for near, group in ((1, 3), (2, 2)):

            @pl.when(plane != near)
            def _():
                pass_on(group, pos)

    @pl.loop(0, n)
    def _(q):
        arrived(sm.at[q], pr.at[0, q])
        arrived(ft.at[rows(q, un)], pr.at[1, q])

    for q in range(n):
        block = sm[q, 0:SMALL, :]
        v1[:, q * dn : (q + 1) * dn] = block[0:8]
        for r in range(3):
            at = slice((3 * q + r) * dn, (3 * q + r + 1) * dn)
            bi[0:1, at] = block[7 + r : 8 + r]
            for tap in range(3):
                ks[tap : tap + 1, at] = block[10 + 3 * tap + r : 11 + 3 * tap + r]
        for r in range(wide):
            at = slice((wide * q + r) * dn, (wide * q + r + 1) * dn)
            bu[0:1, at] = block[19 + r : 20 + r]
        tw[:, q * dn : (q + 1) * dn] = sm[q, SMALL : SMALL + units, :]

    lane = lax.broadcasted_iota(jnp.int32, (lags, 2 * units), 1)
    embed, deep = ft[:, 0:128], ft[:, 128:256]
    pre1 = lax.dot_general(
        table[...], embed, (((1,), (1,)), ((), ())), precision=HIGH, preferred_element_type=F32
    )
    one = jnp.where(lane == units, 1.0, jnp.sin(pre1))
    pre2 = lax.dot_general(
        one, deep, (((1,), (1,)), ((), ())), precision=HIGH, preferred_element_type=F32
    )
    two = jnp.sin(pre2)
    fstate[0] = one
    fstate[1] = jnp.cos(pre1)
    fstate[2] = two
    fstate[3] = jnp.cos(pre2)
    taps[...] = (
        jnp.dot(two[:, 0:units], tw[...], precision=HIGH, preferred_element_type=F32) * decay[...]
    )

    @pl.loop(0, PLANES)
    def _(q):
        arrived(bm.at[rows(q, MT)], mr.at[q])

    def share_copy(pos, q):
        at = held_at(pos, q, k)
        return remote(at, at, fs.at[pos, q], fr.at[pos, q], other, z)

    @pl.loop(0, n)
    def _(q):
        for pos in range(pieces):
            arrived(held_at(pos, q, k), wr.at[pos, q])
            share_copy(pos, q).start()

    @pl.loop(0, n)
    def _(q):
        for pos in range(pieces):
            share_copy(pos, q).wait()

    CB = 256
    UB = 512
    per = D // UB

    def spread(block, width):
        return jnp.concatenate([block] * (width // 128), axis=1)

    def hop_forward(b, part):
        at, col = rows(b, MT), pl.ds(part * HW, HW)
        return remote(
            s_out.at[at, col], s_in.at[at, col], hfs.at[b, part], hfr.at[b, part], next_s, next_z
        )

    def give_out(b):
        return (
            s_out.at[rows(b, MT)],
            r_out.at[rows(k, MT)],
            sos.at[b],
            sor.at[k],
            own_s,
            PLANES * rho + b,
            own_e == 1,
        )

    def give_grad(b):
        return (
            g_out.at[rows(b, MT)],
            r_grad.at[rows(k, MT)],
            sgs.at[b],
            sgr.at[k],
            own_s,
            PLANES * rho + b,
            own_e == 0,
        )

    halves = ((xn, pxn, D // 2), (xg, pxg, D // 2), (x2, px2, D // 2), (xa, pxa, FF // 2))

    def swap_left(b, pos):
        src, dst, width = halves[pos]
        at = rows(b, MT)
        return remote(
            src.at[at, rows(1 - k, width)], dst.at[at], xs.at[pos, b], xr.at[pos, b], other, z
        )

    fulls = ((dp, pdp), (dg, pdg), (dh, pdh), (g_arr, pdm))

    def swap_right(b, pos):
        src, dst = fulls[pos]
        at = rows(b, MT)
        return remote(src.at[at], dst.at[at], ds.at[pos, b], dr.at[pos, b], other, z)

    @pl.when(jnp.logical_and(first, k == 0))
    def _():
        pl.semaphore_signal(lag_sem, inc=1, device_id=(other, z), device_id_type=MESH)

    @pl.when(jnp.logical_and(first, k == 1))
    def _():
        pl.semaphore_wait(lag_sem, 1)

    @pl.loop(0, m)
    def _(b):
        at = rows(b, MT)
        for part in range(HOPS):
            arrived(s_in.at[at, pl.ds(part * HW, HW)], hfr.at[b, part])
        stream = s_in[at, :].astype(F32)
        unit, _ = norm_parts(stream)
        normed = (unit * v1[0:1, :] + v1[1:2, :]).astype(BF16)
        xn[at, :] = normed
        bb = spread(bm[at, :], CB)
        for cb in range(D // CB):
            col = slice(cb * CB, (cb + 1) * CB)
            parts = []
            for group in range(3):
                wcol = slice(group * D + cb * CB, group * D + (cb + 1) * CB)
                p = dot_rows(normed, w[group, :, col]) + bi[0:1, wcol]
                y1 = bb * pltpu.roll(p, 1, 0)
                y2 = bb * pltpu.roll(y1, 1, 0)
                out = ks[0:1, wcol] * p + ks[1:2, wcol] * y1 + ks[2:3, wcol] * y2
                proj[at, wcol] = p
                conv[at, wcol] = out
                parts.append(out)
            mixed = parts[2] * parts[1]
            total = (v1[2:3, col] + taps[0:1, col]) * mixed
            moved = mixed
            for lag in range(1, lags):
                moved = bb * pltpu.roll(moved, 1, 0)
                total = total + taps[lag : lag + 1, col] * moved
            lcs[at, col] = total
            xg[at, col] = (total * parts[0]).astype(BF16)
        gated = xg[at, :]
        for cb in range(D // CB):
            col = slice(cb * CB, (cb + 1) * CB)
            mid[at, col] = (
                s_in[at, col].astype(F32)
                + dot_rows(gated, w[3, :, col])
                + v1[3:4, col]
            )
        unit, _ = norm_parts(mid[at, :])
        second = (unit * v1[4:5, :] + v1[5:6, :]).astype(BF16)
        x2[at, :] = second
        for ub in range(FF // UB):
            col = slice(ub * UB, (ub + 1) * UB)
            wcol = slice((ub % per) * UB, (ub % per + 1) * UB)
            before = (
                dot_rows(second, w[4 + ub // per, :, wcol]) + bu[0:1, col]
            )
            phi = 0.5 + 0.5 * lax.erf(before * (1.0 / math.sqrt(2.0)))
            dens = jnp.exp(-0.5 * before * before) * (1.0 / math.sqrt(2.0 * math.pi))
            gpr[at, col] = phi + before * dens
            xa[at, col] = (before * phi).astype(BF16)
        for part in range(HOPS):
            col = slice(part * HW, (part + 1) * HW)
            total = mid[at, col] + v1[6:7, col]
            for q in range(wide):
                total = total + dot_rows(xa[at, q * D : (q + 1) * D], w[blocks + q, :, col])
            s_out[at, col] = total.astype(BF16)

            @pl.when(jnp.logical_not(last))
            def _():
                hop_forward(b, part).start()

        start(*give_out(b))
        for pos in range(4):
            swap_left(b, pos).start()

    TB = 256

    @pl.loop(0, blocks + wide)
    def _(b):
        for top in range(D // TB):
            up = slice(top * TB, (top + 1) * TB)
            w[b, up, up] = w[b, up, up].T
            for low in range(top + 1, D // TB):
                down = slice(low * TB, (low + 1) * TB)
                one, two = w[b, up, down], w[b, down, up]
                w[b, up, down] = two.T
                w[b, down, up] = one.T

    def hop_back(b):
        at = rows(b, MT)
        return remote(g_out.at[at], g_arr.at[at], hbs.at[b], hbr.at[b], prev_s, prev_z)

    @pl.when(jnp.logical_and(last, k == 0))
    def _():
        pl.semaphore_signal(lag_sem, inc=1, device_id=(other, z), device_id_type=MESH)

    @pl.when(jnp.logical_and(last, k == 1))
    def _():
        pl.semaphore_wait(lag_sem, 1)

    @pl.loop(0, m)
    def _(b):
        at = rows(b, MT)
        arrived(g_arr.at[at], hbr.at[b])
        swap_right(b, 3).start()
        low = g_arr[at, :]
        grad = low.astype(F32)
        a1[6] += fold(grad)
        for ub in range(FF // UB):
            col = slice(ub * UB, (ub + 1) * UB)
            wcol = slice((ub % per) * UB, (ub % per + 1) * UB)
            inner = (
                dot_rows(low, w[blocks + ub // per, :, wcol])
                * gpr[at, col]
            )
            abu[:, col] += fold(inner)
            dh[at, col] = inner.astype(BF16)
        swap_right(b, 2).start()

        def times(left, begin, count):
            parts = []
            for cb in range(D // CB):
                col = slice(cb * CB, (cb + 1) * CB)
                parts.append(
                    sum(
                        dot_rows(left[at, q * D : (q + 1) * D], w[begin + q, :, col])
                        for q in range(count)
                    )
                )
            return jnp.concatenate(parts, axis=1)

        grad2 = times(dh, 4, wide)
        unit, rate = norm_parts(mid[at, :])
        a1[4] += fold(grad2 * unit)
        a1[5] += fold(grad2)
        middle = grad + norm_back(grad2, v1[4:5, :], unit, rate)
        a1[3] += fold(middle)
        mid[at, :] = middle
        low = middle.astype(BF16)
        dg[at, :] = low
        swap_right(b, 1).start()
        bb = bm[at, :]
        bb = spread(pltpu.roll(bb, MT - 1, 0), CB)
        for cb in range(D // CB):
            col = slice(cb * CB, (cb + 1) * CB)
            gg = dot_rows(low, w[3, :, col])
            cols = [slice(g * D + cb * CB, g * D + (cb + 1) * CB) for g in range(3)]
            c_out, c_in, c_val = (conv[at, item] for item in cols)
            d_out = gg * lcs[at, col]
            moved = gg * c_out
            mixed = c_in * c_val
            direct = fold(moved * mixed)
            a1[2, :, col] += direct
            atp[0, :, col] += direct
            total = (v1[2:3, col] + taps[0:1, col]) * moved
            for lag in range(1, lags):
                moved = bb * pltpu.roll(moved, MT - 1, 0)
                total = total + taps[lag : lag + 1, col] * moved
                atp[lag, :, col] += fold(moved * mixed)
            for item, piece in zip(cols, (d_out, total * c_val, total * c_in)):
                z1 = bb * pltpu.roll(piece, MT - 1, 0)
                z2 = bb * pltpu.roll(z1, MT - 1, 0)
                p = proj[at, item]
                whole = ks[0:1, item] * piece + ks[1:2, item] * z1 + ks[2:3, item] * z2
                aks[0, :, item] += fold(p * piece)
                aks[1, :, item] += fold(p * z1)
                aks[2, :, item] += fold(p * z2)
                abi[:, item] += fold(whole)
                dp[at, item] = whole.astype(BF16)
        swap_right(b, 0).start()
        grad1 = times(dp, 0, 3)
        unit, rate = norm_parts(s_in[at, :].astype(F32))
        a1[0] += fold(grad1 * unit)
        a1[1] += fold(grad1)
        g_out[at, :] = (mid[at, :] + norm_back(grad1, v1[0:1, :], unit, rate)).astype(BF16)

        @pl.when(jnp.logical_not(first))
        def _():
            hop_back(b).start()

        start(*give_grad(b))

    @pl.loop(0, m)
    def _(b):
        for pos in range(4):
            swap_left(b, pos).wait()
            swap_right(b, pos).wait()

    def made_at(pos, q):
        if pos < blocks:
            return pos, q * dn
        return blocks + div(q * fn, D), rem(q * fn, D)

    def home_at(e, copy, pos):
        if pos < 3:
            return g_in_w.at[e, copy, :, pl.ds(pos * D, D)]
        if pos == 3:
            return g_out_w.at[e, copy]
        if pos < blocks:
            return g_up_w.at[e, copy, :, pl.ds((pos - 4) * D, D)]
        return g_down_w.at[e, copy]

    def back_at(group, copy, pos):
        return back.at[group, copy, pos] if pos < blocks else back_down.at[group, copy]

    own_group = div(layer, C)
    relayed = own_group >= 2

    def made(pos, half):
        q = k * (n // 2) + half
        block, begin = made_at(pos, q)
        share = dn if pos < blocks else fn
        return q, w.at[block, pl.ds(pl.multiple_of(begin, share), share)]

    def relay_copy(pos, half):
        q, src = made(pos, half)
        to = jnp.maximum(own_group - 2, 0)
        return (
            src,
            back_at(to, rho, pos),
            gs.at[pos, half],
            br.at[to, rho, pos],
            2 * c + rem(own_s, 2),
            q,
            relayed,
        )

    def direct_copy(pos, half):
        q, src = made(pos, half)
        return (
            src,
            home_at(own_e, rho, pos),
            gs.at[pos, half],
            gr.at[pos, own_e, rho],
            own_s,
            q,
            jnp.logical_not(relayed),
        )

    def home_copy(group, copy, pos):
        lay = layer_of(c, jnp.int32((group + 3) % PLANES), C)
        to_s, e = div(lay, 2), rem(lay, 2)
        mine = rem(to_s, 2) == k
        return mine, (
            back_at(group, copy, pos),
            home_at(e, copy, pos),
            bs.at[group, copy, pos],
            gr.at[pos, e, copy],
            to_s,
            z,
        )

    RB = min(256, dn)

    for pos in reversed(range(pieces)):

        @pl.loop(0, n // 2)
        def _(turn):
            half = rem(turn + c, n // 2)
            q = k * (n // 2) + half
            kind = 0 if pos < 3 else 1 if pos == 3 else 2 if pos < blocks else 3
            left = (xn, xg, x2, xa)[kind]
            left2 = (pxn, pxg, px2, pxa)[kind]
            right, right2 = fulls[kind]
            begin_col = (pos, 0, pos - 4, 0)[kind] * D
            col = slice(begin_col, begin_col + D)
            share = dn if pos < blocks else fn
            block, begin = made_at(pos, q)

            @pl.loop(0, share // RB)
            def _(t):
                mine = left[:, pl.ds(pl.multiple_of(q * share + t * RB, RB), RB)]
                theirs = left2[:, pl.ds(pl.multiple_of(half * share + t * RB, RB), RB)]
                at = pl.ds(pl.multiple_of(begin + t * RB, RB), RB)
                w[block, at, :] = (
                    dot_tokens(mine, right[:, col]) + dot_tokens(theirs, right2[:, col])
                ).astype(BF16)

            start(*relay_copy(pos, half))
            start(*direct_copy(pos, half))

    def total(value):
        return jnp.sum(value, axis=0, keepdims=True)

    dt = jnp.concatenate([total(atp[lag]) for lag in range(lags)], axis=0) * decay[...]
    one, cos1, two, cos2 = (fstate[index] for index in range(4))
    d_tw = dot_tokens(two[:, 0:units], dt, HIGH)
    tw2 = jnp.concatenate([tw[...], jnp.zeros_like(tw)], axis=0)
    d_two = (
        lax.dot_general(dt, tw2, (((1,), (1,)), ((), ())), precision=HIGH, preferred_element_type=F32)
        * cos2
    )
    d_deep = dot_tokens(d_two, one, HIGH)
    d_one = jnp.dot(d_two, ft[:, 128:256], precision=HIGH, preferred_element_type=F32) * cos1
    d_one = jnp.where(lane < units, d_one, 0.0)
    fgrad[:, 0:128] = dot_tokens(d_one, table[...], HIGH)
    fgrad[:, 128:256] = d_deep
    vec = [total(a1[index]) for index in range(7)]
    bias, bias_up = total(abi[...]), total(abu[...])
    taps3 = [total(aks[tap]) for tap in range(3)]
    for q in range(n):
        at = slice(q * dn, (q + 1) * dn)
        for index in range(7):
            sgrad[q, index : index + 1, :] = vec[index][:, at]
        for r in range(3):
            wide_at = slice((3 * q + r) * dn, (3 * q + r + 1) * dn)
            sgrad[q, 7 + r : 8 + r, :] = bias[:, wide_at]
            for tap in range(3):
                row = 10 + 3 * tap + r
                sgrad[q, row : row + 1, :] = taps3[tap][:, wide_at]
        for r in range(wide):
            wide_at = slice((wide * q + r) * dn, (wide * q + r + 1) * dn)
            sgrad[q, 19 + r : 20 + r, :] = bias_up[:, wide_at]
        sgrad[q, SMALL : SMALL + units, :] = d_tw[:, at]

    def vector_copies(q):
        slot = 2 * rho + k
        yield (sgrad.at[q], g_small.at[own_e, slot], vs.at[0, q], vr.at[0, own_e, slot], own_s, q)
        yield (
            fgrad.at[rows(q, un)],
            g_filt.at[own_e, slot],
            vs.at[1, q],
            vr.at[1, own_e, slot],
            own_s,
            q,
        )

    @pl.loop(0, n)
    def _(q):
        for copy in vector_copies(q):
            start(*copy)

    for group in (1, 0):
        for copy in range(R):
            for pos in reversed(range(pieces)):
                mine, args = home_copy(group, copy, pos)

                @pl.when(mine)
                def _():
                    arrived(back_at(group, copy, pos), br.at[group, copy, pos])

                start(*args, mine)

    for copy in token_copies():
        sent(*copy)
    for copy in column_copies():
        sent(*copy)
    for copy in small_copies():
        sent(*copy)
    for group in range(PLANES):
        for pos in range(pieces):
            for copy in plane_copies(group, pos):
                sent(*copy)

    @pl.loop(0, m)
    def _(b):
        @pl.when(jnp.logical_not(last))
        def _():
            for part in range(HOPS):
                hop_forward(b, part).wait_send()

        @pl.when(jnp.logical_not(first))
        def _():
            hop_back(b).wait_send()

        sent(*give_out(b))
        sent(*give_grad(b))

    @pl.loop(0, n)
    def _(q):
        for copy in vector_copies(q):
            sent(*copy)

    @pl.loop(0, n // 2)
    def _(half):
        for pos in range(pieces):
            sent(*relay_copy(pos, half))
            sent(*direct_copy(pos, half))

    for group in range(2):
        for copy in range(R):
            for pos in range(pieces):
                mine, args = home_copy(group, copy, pos)
                sent(*args, mine)

    for core in range(2):
        arrived(r_out.at[rows(jnp.int32(core), MT)], sor.at[core])
        arrived(r_grad.at[rows(jnp.int32(core), MT)], sgr.at[core])

    @pl.loop(0, 2)
    def _(e):
        for slot in range(2 * R):
            arrived(g_small.at[e, slot], vr.at[0, e, slot])
            arrived(g_filt.at[e, slot], vr.at[1, e, slot])
        for copy in range(R):
            for pos in range(pieces):
                arrived(home_at(e, copy, pos), gr.at[pos, e, copy])


def constants(length, width, lags):
    steps = np.arange(lags, dtype=np.float32)
    bands = np.arange(1, 17, dtype=np.float32)
    angles = np.float32(2.0 * np.pi) * steps[:, None] * bands[None, :] / np.float32(length)
    table = np.zeros((lags, 128), np.float32)
    table[:, 0] = steps / length
    table[:, 1:17] = np.cos(angles)
    table[:, 17:33] = np.sin(angles)
    table[:, 33] = 1.0
    rates = np.exp(np.linspace(math.log(0.3), math.log(30.0), width)).astype(np.float32)
    decay = np.exp(-(steps / np.float32(length))[:, None] * rates[None, :]).astype(np.float32)
    return table, decay


def on_device(
    S,
    n,
    tokens,
    cotangent,
    lengths,
    mixer_gain,
    mixer_shift,
    input_weight,
    input_bias,
    short_kernel,
    embed_weight,
    embed_bias,
    filter_weight,
    filter_bias,
    taps_weight,
    skip_gain,
    output_weight,
    output_bias,
    feed_gain,
    feed_shift,
    up_weight,
    up_bias,
    down_weight,
    down_bias,
):
    micro, length, D = tokens.shape
    FF = up_weight.shape[-1]
    dn = mixer_gain.shape[-1]
    units = filter_weight.shape[1]
    un = units // n
    emb = embed_weight.shape[1]
    R = n // PLANES
    m = PLANES
    MT = micro * length // 2
    TT = m * MT
    lags = length // 2
    wide = FF // D

    table, decay = constants(length, D, lags)

    hbm = pl.BlockSpec(memory_space=pl.ANY)
    vmem = pl.BlockSpec(memory_space=pltpu.VMEM)
    smem = pl.BlockSpec(memory_space=pltpu.SMEM)
    dma = pltpu.SemaphoreType.DMA
    blocks = 4 + wide
    pieces = blocks + 1
    out_shape = (
        jax.ShapeDtypeStruct((2, R, dn, 3 * D), BF16),
        jax.ShapeDtypeStruct((2, R, dn, D), BF16),
        jax.ShapeDtypeStruct((2, R, dn, FF), BF16),
        jax.ShapeDtypeStruct((2, R, FF // n, D), BF16),
        jax.ShapeDtypeStruct((2, 2 * R, SMALL + units, dn), F32),
        jax.ShapeDtypeStruct((2, 2 * R, un, 256), F32),
        jax.ShapeDtypeStruct((2 * MT, D), BF16),
        jax.ShapeDtypeStruct((2 * MT, D), BF16),
        jax.ShapeDtypeStruct((PLANES, blocks, dn // 2, D), BF16),
        jax.ShapeDtypeStruct((PLANES, FF // n // 2, D), BF16),
        jax.ShapeDtypeStruct((2, R, blocks, dn, D), BF16),
        jax.ShapeDtypeStruct((2, R, FF // n, D), BF16),
    )
    V = pltpu.VMEM
    scratch = [
        V((blocks + wide, D, D), BF16),
        V((n, SMALL + units, dn), F32),
        V((2 * units, 256), F32),
        V((2, SMALL + units, dn), F32),
        V((2, un, 256), F32),
        V((MT, 128), F32),
        V((128, 128), F32),
        V((8, D), F32),
        V((8, 3 * D), F32),
        V((8, 3 * D), F32),
        V((8, FF), F32),
        V((units, D), F32),
        V((lags, D), F32),
        V((4, lags, 2 * units), F32),
        V((TT, 128), F32),
        V((TT, D), BF16),
        V((TT, D), BF16),
        V((TT, D), BF16),
        V((TT, D), BF16),
        V((TT, D), BF16),
        V((TT, D), BF16),
        V((TT, D), BF16),
        V((TT, FF), BF16),
        V((TT, 3 * D), F32),
        V((TT, 3 * D), F32),
        V((TT, D), F32),
        V((TT, FF), F32),
        V((TT, D), F32),
        V((TT, 3 * D), BF16),
        V((TT, D), BF16),
        V((TT, FF), BF16),
        V((TT, D // 2), BF16),
        V((TT, D // 2), BF16),
        V((TT, D // 2), BF16),
        V((TT, FF // 2), BF16),
        V((TT, 3 * D), BF16),
        V((TT, D), BF16),
        V((TT, FF), BF16),
        V((TT, D), BF16),
        V((7, 8, D), F32),
        V((8, 3 * D), F32),
        V((3, 8, 3 * D), F32),
        V((8, FF), F32),
        V((lags, 8, D), F32),
        V((n, SMALL + units, dn), F32),
        V((2 * units, 256), F32),
        dma((2, 2, pieces)),
        dma((PLANES, pieces)),
        dma((PLANES, R, pieces)),
        dma((pieces, n)),
        dma((pieces, n)),
        dma((pieces, n)),
        dma((2, 2, R, 2)),
        dma((2, n)),
        dma((PLANES,)),
        dma((PLANES,)),
        dma((HOPS,)),
        dma((1,)),
        dma((m, HOPS)),
        dma((m, HOPS)),
        dma((m,)),
        dma((m,)),
        dma((m,)),
        dma((2,)),
        dma((m,)),
        dma((2,)),
        dma((4, m)),
        dma((4, m)),
        dma((4, m)),
        dma((4, m)),
        dma((pieces, n // 2)),
        dma((pieces, 2, R)),
        dma((2, R, pieces)),
        dma((2, R, pieces)),
        dma((2, n)),
        dma((2, 2, 2 * R)),
        pltpu.SemaphoreType.REGULAR,
    ]
    size = (S, n, R, D, FF, m, MT, lags, units, length)
    gi, go, gu, gd, gsm, gft, r_out, r_grad, *_ = pl.pallas_call(
        functools.partial(kernel, size),
        out_shape=out_shape,
        in_specs=[hbm] * 6 + [smem] + [vmem] * 17,
        out_specs=(hbm,) * 12,
        scratch_shapes=scratch,
        compiler_params=pltpu.CompilerParams(
            collective_id=0, has_side_effects=True, vmem_limit_bytes=62 << 20
        ),
        name="window",
    )(
        tokens.reshape(micro * length, D),
        cotangent.reshape(micro * length, D),
        input_weight,
        output_weight,
        up_weight,
        down_weight,
        lengths,
        mixer_gain,
        mixer_shift,
        skip_gain,
        output_bias,
        feed_gain,
        feed_shift,
        down_bias,
        input_bias,
        short_kernel,
        up_bias,
        taps_weight,
        embed_weight,
        embed_bias,
        filter_weight,
        filter_bias,
        jnp.asarray(decay),
        jnp.asarray(table),
    )

    def whole(piece):
        return jnp.sum(piece.astype(F32), axis=1)

    vectors = jnp.sum(gsm, axis=1)
    nets = jnp.sum(gft, axis=1)

    def take(begin, count=1):
        return vectors[:, begin : begin + count].reshape(2, count * dn)

    def stream(piece):
        return piece.astype(F32).reshape(1, micro, length, D)

    return (
        stream(r_out),
        stream(r_grad),
        take(0),
        take(1),
        whole(gi),
        take(7, 3),
        vectors[:, 10:19].reshape(2, 3, 3 * dn),
        nets[:, :, 0:emb].transpose(0, 2, 1),
        nets[:, :, emb],
        nets[:, :, 128 : 128 + units].transpose(0, 2, 1),
        nets[:, :, 128 + units],
        vectors[:, SMALL:],
        take(2),
        whole(go),
        take(3),
        take(4),
        take(5),
        whole(gu),
        take(19, wide),
        whole(gd),
        take(6),
    )


def solution(mesh):
    S, n = mesh.shape["section"], mesh.shape["dp"]
    vector, matrix, columns = P("section", "dp"), P("section", "dp", None), P("section", None, "dp")
    weights = (
        vector,
        vector,
        matrix,
        vector,
        columns,
        columns,
        vector,
        columns,
        vector,
        columns,
        vector,
        matrix,
        vector,
        vector,
        vector,
        matrix,
        vector,
        matrix,
        vector,
    )
    rows = P("section", "dp", None, None)
    return jax.shard_map(
        functools.partial(on_device, S, n),
        mesh=mesh,
        in_specs=(P("dp", None, None), P("dp", None, None), P("dp", None)) + weights,
        out_specs=(rows, rows) + weights,
        check_vma=False,
    )
```
